256 devices in a mesh: section: 8 (over z), dp: 8 (over y, core), vocab: 4 (over x).
Axes of the slice: x: 4, y: 4, z: 8, core: 2. Of those that a mesh axis runs over, the one named last changes fastest.
Arguments:
- tokens_in: int32 [32], replicated, may hold values from 0 to 65535
- picks: int32 [1, 32], replicated, may hold values from 0 to 65535
- parents: int32 [1, 32], replicated, may hold values from 0 to 7
- scores: float32 [32], replicated, may hold values from -4 to 4
- embed: bfloat16 [65536, 4096], P('section', ('dp', 'vocab')), may hold values from -6 to 6
- norm_gain: float32 [8, 4096], P('section', ('dp', 'vocab')), may hold values from 0.5 to 1.5
- in_weight: bfloat16 [8, 4096, 2, 4096], P('section', ('dp', 'vocab')), may hold values from -0.09375 to 0.09375
- conv_weight: float32 [8, 4, 4096], P('section', None, 'vocab'), may hold values from -3 to 3
- conv_bias: float32 [8, 4096], P('section', 'vocab'), may hold values from -3 to 3
- xdt_weight: bfloat16 [8, 4096, 256], P('section', 'vocab'), may hold values from -0.09375 to 0.09375
- xbc_weight: bfloat16 [8, 4096, 32], P('section', 'vocab'), may hold values from -0.09375 to 0.09375
- dt_weight: bfloat16 [8, 256, 4096], P('section', None, 'vocab'), may hold values from -0.375 to 0.375
- dt_bias: float32 [8, 4096], P('section', 'vocab'), may hold values from -4 to -1
- a_rate: float32 [8, 16, 4096], P('section', None, 'vocab'), may hold values from 0.5 to 16
- skip: float32 [8, 4096], P('section', 'vocab'), may hold values from 0.1 to 1.9
- out_weight: bfloat16 [8, 4096, 4096], P('section', None, ('dp', 'vocab')), may hold values from -0.09375 to 0.09375
- final_gain: float32 [4096], replicated, may hold values from 0.5 to 1.5
- head: bfloat16 [65536, 4096], P(('section', 'dp', 'vocab'))
- conv_state: bfloat16 [8, 32, 3, 4096], P('section', 'dp', None, 'vocab'), may hold values from -6 to 6
- ssm_state: float32 [8, 32, 16, 4096], P('section', 'dp', None, 'vocab'), may hold values from -6 to 6
Outputs:
- conv_out: bfloat16 [8, 32, 3, 4096], P('section', 'dp', None, 'vocab')
- ssm_out: float32 [8, 32, 16, 4096], P('section', 'dp', None, 'vocab')
- final_scores: float32 [32], replicated
The draws below stay inside these ranges and needn't reach their ends.
Inputs may be any that keep to these rules, and one draw needn't show every extreme that they name: parents[k, g] is a beam number of the source of row g.
All inputs are finite; a program needn't handle non-finite values.
Results may differ from the reference program's by a relative error of at most 0.015.
Values may be sent and summed in bfloat16 or wider, within the bound.
No kernel may reach another device: no remote copies, remote signals or barrier semaphores. Data moves between devices by JAX's collectives and lax.ppermute only.
A program may use at most 128 MiB of HBM per device.

```python
import math
import jax
import jax.numpy as jnp
import numpy as np
from jax import lax

D = 4096
VOCAB = 65536
INNER = 4096
RANK = 256
STATE_DIM = 16
CONV_WIDTH = 4
BEAMS = 8
STEPS = 1
SOURCES = 4
LAYERS = 8
ROWS = 32


def draw_head(key, part):
    key = jax.random.fold_in(key, 11)
    values = jax.random.normal(key, (VOCAB, D), jnp.float32) * (3.0 / math.sqrt(D))
    return values.astype(jnp.bfloat16)


def plant(values, key, smallest, top_value):
    place = [jax.random.randint(jax.random.fold_in(key, axis), (), 0, length) for axis, length in enumerate(values.shape)]
    main_axis = values.shape.index(max(values.shape))
    beside = place[:main_axis] + [(place[main_axis] + 1) % values.shape[main_axis]] + place[main_axis + 1:]
    return values.at[tuple(place)].set(smallest).at[tuple(beside)].set(top_value)


def level_of(stream_key, dims, pieces, least, top_value):
    level, own = 1.0, jax.random.fold_in(stream_key, 6)
    for position, blocks in pieces:
        draws = jnp.exp(jax.random.uniform(jax.random.fold_in(own, position), (blocks,), jnp.float32, least / len(pieces), top_value / len(pieces)))
        level = level * jnp.repeat(draws, dims[position] // blocks).reshape([-1 if axis == position else 1 for axis in range(len(dims))])
    return level


def rank_bounds(number_of, lean):
    portions = [(1 << 20) // math.isqrt(standing ** lean) + 1 for standing in range(1, number_of + 1)]
    deviation = 1 + sum(portions) // (1 << 30)
    return np.cumsum(np.array([max(1, weight // deviation) for weight in portions]))


def ranked(key, dims, count, slope):
    table = rank_bounds(count, slope)
    lot = jax.random.randint(jax.random.fold_in(key, 1), dims, 0, int(table[count - 1]))
    standing = jnp.searchsorted(jnp.asarray(table, jnp.int32), lot, side="right")
    return jax.random.permutation(jax.random.fold_in(key, 2), count)[standing].astype(jnp.int32)


def noise(rng, extent, scale, reach, shards=(), held_as=jnp.bfloat16):
    drawn = scale * jax.random.normal(rng, extent, jnp.float32)
    if shards:
        drawn = drawn * level_of(rng, extent, shards, -0.22, 0.18)
    return jnp.clip(drawn, -reach, reach).astype(held_as)


def setup_inputs(seed: int = 0) -> dict:
    key_of = jax.random.split(jax.random.key(seed), 21)
    tokens_in = plant(jax.random.randint(key_of[0], (ROWS,), 0, VOCAB), jax.random.fold_in(key_of[0], 1), 0, VOCAB - 1).astype(jnp.int32)
    picks = plant(jax.random.randint(key_of[1], (STEPS, ROWS), 0, VOCAB), jax.random.fold_in(key_of[1], 1), 0, VOCAB - 1).astype(jnp.int32)
    parents = plant(ranked(key_of[2], (STEPS, ROWS), BEAMS, 1), jax.random.fold_in(key_of[2], 3), 0, BEAMS - 1).astype(jnp.int32)
    scores = noise(key_of[3], (ROWS,), 1.0, 4.0, (), jnp.float32)
    embed = noise(key_of[4], (VOCAB, D), 1.0, 6.0, ((0, 8), (1, 32)))
    norm_gain = jnp.clip(1.0 + 0.1 * jax.random.normal(key_of[5], (LAYERS, D), jnp.float32), 0.5, 1.5)
    in_weight = noise(key_of[6], (LAYERS, D, 2, INNER), D ** -0.5, 0.09375, ((0, 8), (1, 32)))
    conv_weight = noise(key_of[7], (LAYERS, CONV_WIDTH, INNER), 0.5, 3.0, ((0, 8), (2, 4)), jnp.float32)
    conv_bias = noise(key_of[8], (LAYERS, INNER), 0.5, 3.0, ((0, 8), (1, 4)), jnp.float32)
    xdt_weight = noise(key_of[9], (LAYERS, INNER, RANK), INNER ** -0.5, 0.09375, ((0, 8), (1, 4)))
    xbc_weight = noise(key_of[10], (LAYERS, INNER, 2 * STATE_DIM), INNER ** -0.5, 0.09375, ((0, 8), (1, 4)))
    dt_weight = noise(key_of[11], (LAYERS, RANK, INNER), RANK ** -0.5, 0.375, ((0, 8), (2, 4)))
    dt_bias = jnp.clip(-4.0 + 3.0 * jax.random.uniform(key_of[12], (LAYERS, INNER), jnp.float32) ** level_of(key_of[12], (LAYERS, INNER), ((0, 8), (1, 4)), -0.2, 0.2), -4.0, -1.0)
    a_rate = jnp.clip(jnp.exp(math.log(16.0) - 3.465736 * jax.random.uniform(key_of[13], (LAYERS, STATE_DIM, INNER), jnp.float32) ** level_of(key_of[13], (LAYERS, STATE_DIM, INNER), ((0, 8), (2, 4)), -0.2, 0.2)), 0.5, 16.0)
    skip = jnp.clip(1.0 + 0.18 * jax.random.normal(key_of[14], (LAYERS, INNER), jnp.float32), 0.1, 1.9)
    out_weight = noise(key_of[15], (LAYERS, INNER, D), INNER ** -0.5, 0.09375, ((0, 8), (2, 32)))
    final_gain = jnp.clip(1.0 + 0.1 * jax.random.normal(key_of[16], (D,), jnp.float32), 0.5, 1.5)
    head = draw_head(jax.random.fold_in(key_of[20], 71), 0)
    conv_state = noise(key_of[18], (LAYERS, ROWS, CONV_WIDTH - 1, INNER), 1.0, 6.0, ((0, 8), (1, 8), (3, 4)))
    ssm_state = noise(key_of[19], (LAYERS, ROWS, STATE_DIM, INNER), 1.0, 6.0, ((0, 8), (1, 8), (3, 4)), jnp.float32)
    return dict(tokens_in=tokens_in, picks=picks, parents=parents, scores=scores, embed=embed, norm_gain=norm_gain, in_weight=in_weight, conv_weight=conv_weight, conv_bias=conv_bias, xdt_weight=xdt_weight, xbc_weight=xbc_weight, dt_weight=dt_weight, dt_bias=dt_bias, a_rate=a_rate, skip=skip, out_weight=out_weight, final_gain=final_gain, head=head, conv_state=conv_state, ssm_state=ssm_state)


EPSILON = 1e-05

def reference(tokens_in, picks, parents, scores, embed, norm_gain, in_weight, conv_weight, conv_bias, xdt_weight, xbc_weight, dt_weight, dt_bias, a_rate, skip, out_weight, final_gain, head, conv_state, ssm_state):
    source_of = jnp.arange(ROWS, dtype=jnp.int32) % SOURCES
    tokens_now = tokens_in
    conv_now = conv_state
    ssm_now = ssm_state
    scores_now = scores
    for step_idx in range(STEPS):
        hidden = jnp.take(embed, tokens_now, axis=0).astype(jnp.float32)
        conv_list = []
        ssm_list = []
        for layer_idx in range(LAYERS):
            sq_sums = lax.optimization_barrier(jnp.sum(hidden * hidden, axis=1))
            row_scale = lax.rsqrt(sq_sums / D + EPSILON)
            normed = (hidden * norm_gain[layer_idx]).astype(jnp.bfloat16)
            projected = jnp.dot(normed, in_weight[layer_idx].reshape(D, 2 * INNER), preferred_element_type=jnp.float32)
            projected = (projected * row_scale[:, None]).astype(jnp.bfloat16).reshape(ROWS, 2, INNER)
            window = jnp.concatenate([conv_now[layer_idx], projected[:, 0:1, :]], axis=1)
            conv_act = jax.nn.silu(lax.optimization_barrier(jnp.sum(window.astype(jnp.float32) * conv_weight[layer_idx][None], axis=1)) + conv_bias[layer_idx])
            conv_half = conv_act.astype(jnp.bfloat16)
            dt_low = jnp.dot(conv_half, xdt_weight[layer_idx], preferred_element_type=jnp.float32)
            bc_terms = jnp.dot(conv_half, xbc_weight[layer_idx], preferred_element_type=jnp.float32)
            step_size = jax.nn.softplus(jnp.dot(dt_low.astype(jnp.bfloat16), dt_weight[layer_idx], preferred_element_type=jnp.float32) + dt_bias[layer_idx])
            decays = jnp.exp(-step_size[:, None, :] * a_rate[layer_idx][None])
            new_state = decays * ssm_now[layer_idx] + step_size[:, None, :] * bc_terms[:, :STATE_DIM, None] * conv_act[:, None, :]
            mixed = lax.optimization_barrier(jnp.sum(bc_terms[:, STATE_DIM:, None] * new_state, axis=1)) + skip[layer_idx] * conv_act
            mixed = (mixed * jax.nn.silu(projected[:, 1].astype(jnp.float32))).astype(jnp.bfloat16)
            hidden = hidden + jnp.dot(mixed, out_weight[layer_idx], preferred_element_type=jnp.float32)
            conv_list.append(window[:, 1:])
            ssm_list.append(new_state)
        mean_sq = lax.optimization_barrier(jnp.mean(hidden * hidden, axis=1))
        final = (hidden * lax.rsqrt(mean_sq + EPSILON)[:, None] * final_gain).astype(jnp.bfloat16)
        logits = lax.dot_general(final, head, (((1,), (1,)), ((), ())), preferred_element_type=jnp.float32)
        top_logit = lax.optimization_barrier(jnp.max(logits, axis=1))
        exp_total = lax.optimization_barrier(jnp.sum(jnp.exp(logits - top_logit[:, None]), axis=1))
        log_norm = top_logit + jnp.log(exp_total)
        parent_row = (parents[step_idx] * SOURCES + source_of).astype(jnp.int32)
        picked = logits[parent_row, picks[step_idx]]
        scores_now = scores_now[parent_row] + picked - log_norm[parent_row]
        conv_now = jnp.stack(conv_list)[:, parent_row]
        ssm_now = jnp.stack(ssm_list)[:, parent_row]
        tokens_now = picks[step_idx]
    return (conv_now, ssm_now, scores_now)
```

```python
import jax
import jax.numpy as jnp
from jax import lax
from jax.experimental import pallas as pl
from jax.experimental.pallas import tpu as pltpu
from jax.sharding import PartitionSpec as P

STATE_DIM = 16
SOURCES = 4
EPSILON = 1e-05
TAIL = 128

F32 = jnp.float32
BF16 = jnp.bfloat16


def by_vocab(value, by):
    n = lax.axis_size("vocab")
    return lax.ppermute(value, "vocab", [(i, (i + by) % n) for i in range(n)])


def by_y(value, by):
    n = lax.axis_size("dp") // 2
    pairs = [(2 * y + c, 2 * ((y + by) % n) + c) for y in range(n) for c in range(2)]
    return lax.ppermute(value, "dp", pairs)


def other_core(value):
    n = lax.axis_size("dp")
    return lax.ppermute(value, "dp", [(i, i ^ 1) for i in range(n)])


def next_section(value):
    n = lax.axis_size("section")
    return lax.ppermute(value, "section", [(i, (i + 1) % n) for i in range(n)])


def project_in(h_ref, gain_ref, w_own, w_oth, o0, o1, o2, o3, scr):
    hidden = h_ref[...]
    half = w_own.shape[0]
    wide = w_own.shape[1]
    squares = jnp.sum(hidden * hidden, axis=1, keepdims=True)
    normed = (hidden * gain_ref[...]).astype(BF16)
    part = jnp.dot(normed[:, :half], w_own[...], preferred_element_type=F32)
    part = part + jnp.dot(normed[:, half:], w_oth[...], preferred_element_type=F32)
    scr[:, :wide] = part
    high = squares.astype(BF16).astype(F32)
    lane = lax.broadcasted_iota(jnp.int32, (hidden.shape[0], TAIL), 1)
    scr[:, wide:] = jnp.where(lane == 0, high, jnp.where(lane == 1, squares - high, 0.0))
    for k, out in enumerate((o0, o1, o2, o3)):
        rows = out.shape[0]
        out[...] = scr[k * rows : (k + 1) * rows, :].astype(BF16)


def convolve(model_width, a0, a1, a2, a3, pre_ref, tap_ref, w_x, part_ref, act_ref, gate_ref, x_ref):
    total = (
        a0[...].astype(F32) + a1[...].astype(F32) + a2[...].astype(F32) + a3[...].astype(F32)
    )
    wide = total.shape[1] - TAIL
    half = wide // 2
    squares = total[:, wide : wide + 1] + total[:, wide + 1 : wide + 2]
    scale = lax.rsqrt(squares / model_width + EPSILON)
    projected = (total[:, :wide] * scale).astype(BF16)
    x_ref[...] = projected[:, :half]
    x = projected[:, :half].astype(F32)
    z = projected[:, half:].astype(F32)
    act = jax.nn.silu(pre_ref[...] + x * tap_ref[...])
    act_ref[...] = act
    gate_ref[...] = jax.nn.silu(z)
    part_ref[...] = jnp.dot(act.astype(BF16), w_x[...], preferred_element_type=F32)


def advance(
    active_ref, p0, p1, p2, p3, act_ref, gate_ref, w_dt, shift_ref, rate_ref, skip_ref, ssm_in,
    mixed_ref, ssm_out, scr,
):
    terms = p0[...] + p1[...] + p2[...] + p3[...]
    rank = w_dt.shape[0]
    low = terms[:, :rank].astype(BF16)
    pre = jnp.dot(low, w_dt[...], preferred_element_type=F32) + shift_ref[...]
    step = jnp.maximum(pre, 0.0) + jnp.log1p(jnp.exp(-jnp.abs(pre)))
    act = act_ref[...]
    scr[0] = step
    scr[1] = step * act
    bc = terms[:, rank : rank + 2 * STATE_DIM]
    rows = bc.shape[0]
    shape = (STATE_DIM, 2 * STATE_DIM)
    lane = lax.broadcasted_iota(jnp.int32, shape, 1)
    sub = lax.broadcasted_iota(jnp.int32, shape, 0)
    rates = rate_ref[...]
    live = active_ref[0] != 0
    for g in range(rows):
        line = jnp.broadcast_to(bc[g : g + 1, :], shape)
        b_col = jnp.sum(jnp.where(lane == sub, line, 0.0), axis=1, keepdims=True)
        c_col = jnp.sum(jnp.where(lane == sub + STATE_DIM, line, 0.0), axis=1, keepdims=True)
        old = ssm_in[g]
        new = jnp.exp(-scr[0, g : g + 1, :] * rates) * old + b_col * scr[1, g : g + 1, :]
        scr[2, g : g + 1, :] = jnp.sum(c_col * new, axis=0, keepdims=True)
        ssm_out[g] = jnp.where(live, new, old)
    mixed_ref[...] = ((scr[2] + skip_ref[...] * act) * gate_ref[...]).astype(BF16)


def project_out(m0, m1, m2, m3, w_own, w_oth, out_ref, scr):
    for k, ref in enumerate((m0, m1, m2, m3)):
        rows = ref.shape[0]
        scr[k * rows : (k + 1) * rows, :] = ref[...].astype(F32)
    mixed = scr[...].astype(BF16)
    half = w_own.shape[1]
    out_ref[:, :half] = jnp.dot(mixed, w_own[...], preferred_element_type=F32).astype(BF16)
    out_ref[:, half:] = jnp.dot(mixed, w_oth[...], preferred_element_type=F32).astype(BF16)


def local_call(body, outs, scratch=(), smem=0, operands=0, aliases=None, cost=None):
    vmem = pl.BlockSpec(memory_space=pltpu.VMEM)
    specs = [pl.BlockSpec(memory_space=pltpu.SMEM)] * smem + [vmem] * (operands - smem)
    return pl.pallas_call(
        body,
        out_shape=[jax.ShapeDtypeStruct(shape, dtype) for shape, dtype in outs],
        in_specs=specs,
        out_specs=[vmem] * len(outs),
        scratch_shapes=[pltpu.VMEM(shape, F32) for shape in scratch],
        input_output_aliases=aliases or {},
        compiler_params=pltpu.CompilerParams(vmem_limit_bytes=24 * 2**20),
        cost_estimate=cost,
    )


def on_device(
    tokens_in,
    picks,
    parents,
    scores,
    embed,
    norm_gain,
    in_weight,
    conv_weight,
    conv_bias,
    xdt_weight,
    xbc_weight,
    dt_weight,
    dt_bias,
    a_rate,
    skip,
    out_weight,
    final_gain,
    head,
    conv_state,
    ssm_state,
):
    section_count = lax.axis_size("section")
    dp_count = lax.axis_size("dp")
    vocab_count = lax.axis_size("vocab")
    y_count = dp_count // 2
    row_total = tokens_in.shape[0]
    own_rows = row_total // dp_count
    core_rows = own_rows * y_count
    section_at = lax.axis_index("section")
    dp_at = lax.axis_index("dp")
    vocab_at = lax.axis_index("vocab")
    y_at = dp_at // 2
    core_at = dp_at % 2
    block = in_weight.shape[1]
    chan = in_weight.shape[3] // vocab_count
    model_width = final_gain.shape[0]
    core_width = block * vocab_count
    y_width = 2 * core_width
    vocab_rows = head.shape[0]

    w_in = in_weight[0].reshape(block, 2, vocab_count, chan)
    in_blocks = [
        lax.dynamic_index_in_dim(w_in, (vocab_at + k) % vocab_count, 2, keepdims=False).reshape(
            block, 2 * chan
        )
        for k in range(vocab_count)
    ]
    in_blocks = in_blocks[:1] + [by_vocab(in_blocks[k], k) for k in range(1, vocab_count)]
    in_own = jnp.zeros((core_width, 2 * chan), BF16)
    for k in range(vocab_count):
        at = ((vocab_at - k) % vocab_count) * block
        in_own = lax.dynamic_update_slice(in_own, in_blocks[k], (at, 0))
    in_oth = other_core(in_own)

    embed_rows = embed.shape[0]
    local_ids = tokens_in - section_at * embed_rows
    inside = (local_ids >= 0) & (local_ids < embed_rows)
    found = jnp.take(embed, jnp.clip(local_ids, 0, embed_rows - 1), axis=0)
    found = jnp.where(inside[:, None], found, 0).astype(BF16)
    pieces = [lax.ppermute(found, "section", [(k, 0)]) for k in range(1, section_count)]
    looked_up = found.astype(F32)
    for piece in pieces:
        looked_up = looked_up + piece.astype(F32)
    bundle = jnp.concatenate(
        [looked_up, norm_gain, jnp.zeros((7, block), F32)], axis=0
    )
    bundles = [bundle] + [by_vocab(bundle, k) for k in range(1, vocab_count)]
    stacked = jnp.concatenate(bundles[:1] + bundles[:0:-1], axis=0).reshape(
        vocab_count, row_total + 8, block
    )
    stacked = jnp.roll(stacked, vocab_at, axis=0)
    own_part = jnp.transpose(stacked, (1, 0, 2)).reshape(row_total + 8, core_width)
    both = jnp.concatenate([own_part, other_core(own_part)], axis=1)
    gain = both[row_total : row_total + 1]
    hidden = lax.dynamic_index_in_dim(
        both[:row_total].reshape(y_count, 2, own_rows, y_width), core_at, 1, keepdims=False
    )
    hidden = jnp.roll(hidden, -y_at, axis=0).reshape(core_rows, y_width)

    w_out = out_weight[0].reshape(vocab_count, chan, block)
    out_blocks = [
        lax.dynamic_index_in_dim(w_out, (vocab_at + k) % vocab_count, 0, keepdims=False)
        for k in range(vocab_count)
    ]
    out_blocks = out_blocks[:1] + [by_vocab(out_blocks[k], k) for k in range(1, vocab_count)]
    out_own = jnp.zeros((chan, core_width), BF16)
    for k in range(vocab_count):
        at = ((vocab_at - k) % vocab_count) * block
        out_own = lax.dynamic_update_slice(out_own, out_blocks[k], (0, at))
    out_oth = other_core(out_own)

    w_x = jnp.concatenate([xdt_weight[0], xbc_weight[0]], axis=1)
    taps = conv_weight[0]
    conv_old = conv_state[0]
    keep = taps.shape[0] - 1
    conv_pre = conv_bias + jnp.sum(conv_old.astype(F32) * taps[None, :keep], axis=1)
    conv_tap = taps[keep:]
    ssm_now = ssm_state[0]
    x_kept = jnp.zeros((own_rows, chan), BF16)

    wide = 2 * chan + TAIL
    terms_wide = w_x.shape[1]
    call_in = local_call(
        project_in,
        [((own_rows, wide), BF16)] * y_count,
        scratch=[(core_rows, wide)],
        operands=4,
        cost=pl.CostEstimate(
            flops=4 * core_rows * y_width * chan, bytes_accessed=4 * y_width * chan, transcendentals=0
        ),
    )
    call_conv = local_call(
        lambda *refs: convolve(model_width, *refs),
        [
            ((own_rows, terms_wide), F32),
            ((own_rows, chan), F32),
            ((own_rows, chan), F32),
            ((own_rows, chan), BF16),
        ],
        operands=7,
        cost=pl.CostEstimate(
            flops=2 * own_rows * chan * terms_wide,
            bytes_accessed=2 * chan * terms_wide,
            transcendentals=2 * own_rows * chan,
        ),
    )
    call_state = local_call(
        advance,
        [((own_rows, chan), BF16), (ssm_now.shape, F32)],
        scratch=[(3, own_rows, chan)],
        smem=1,
        operands=12,
        aliases={11: 1},
        cost=pl.CostEstimate(
            flops=2 * own_rows * chan * dt_weight.shape[1],
            bytes_accessed=2 * chan * dt_weight.shape[1] + 8 * ssm_now.size,
            transcendentals=ssm_now.size,
        ),
    )
    call_out = local_call(
        project_out,
        [((core_rows, y_width), BF16)],
        scratch=[(core_rows, chan)],
        operands=6,
        cost=pl.CostEstimate(
            flops=2 * core_rows * y_width * chan, bytes_accessed=2 * y_width * chan, transcendentals=0
        ),
    )

    for step in range(section_count):
        active = section_at == step
        parts = list(call_in(hidden, gain, in_own, in_oth))
        parts = parts[:1] + [by_y(parts[k], k) for k in range(1, y_count)]
        terms, act, gate, x_new = call_conv(*parts, conv_pre, conv_tap, w_x)
        x_kept = jnp.where(active, x_new, x_kept)
        all_terms = [terms] + [by_vocab(terms, k) for k in range(1, vocab_count)]
        mixed, ssm_now = call_state(
            active.astype(jnp.int32).reshape(1),
            *all_terms,
            act,
            gate,
            dt_weight[0],
            dt_bias,
            a_rate[0],
            skip,
            ssm_now,
        )
        mixes = [mixed] + [by_y(mixed, -k) for k in range(1, y_count)]
        (added,) = call_out(*mixes, out_own, out_oth)
        total = added.astype(F32)
        for k in range(1, vocab_count):
            total = total + by_vocab(added, k).astype(F32)
        hidden = hidden + total
        if step + 1 < section_count:
            hidden = next_section(hidden)

    natural = jnp.roll(hidden.reshape(y_count, own_rows, y_width), y_at, axis=0)
    natural = natural.reshape(core_rows, 2, core_width)
    natural = jnp.where(core_at == 0, natural, natural[:, ::-1]).reshape(core_rows, y_width)
    squares = jnp.sum(natural * natural, axis=1, keepdims=True)
    high = squares.astype(BF16)
    low = (squares - high.astype(F32)).astype(BF16)
    y_gain = lax.dynamic_slice_in_dim(final_gain, y_at * y_width, y_width, 0)
    sent = jnp.concatenate(
        [(natural * y_gain).astype(BF16), high, low, jnp.zeros((core_rows, TAIL - 2), BF16)], axis=1
    )
    last = section_count - 1
    middle = last // 2
    got = lax.ppermute(sent, "section", [(last, middle)])
    sent = jnp.where(section_at == middle, got, sent)
    received = jnp.zeros_like(sent)
    for k in range(1, middle + 1):
        pairs = [(last, (last + k) % section_count), (middle, middle + k)]
        received = received + lax.ppermute(sent, "section", pairs)
    is_source = (section_at == middle) | (section_at == last)
    sent = jnp.where(is_source, sent, received)
    every_y = jnp.stack([sent] + [by_y(sent, -k) for k in range(1, y_count)])
    every_y = jnp.roll(every_y, y_at, axis=0)
    facing = other_core(every_y)
    cores = jnp.where(core_at == 0, jnp.stack([every_y, facing]), jnp.stack([facing, every_y]))
    cores = cores.reshape(2, y_count, y_count, own_rows, y_width + TAIL)
    cores = jnp.transpose(cores, (2, 0, 3, 1, 4))
    sums = jnp.sum(cores[..., y_width : y_width + 2].astype(F32), axis=(3, 4)).reshape(row_total)
    final = cores[..., :y_width].reshape(row_total, model_width)
    final_scale = lax.rsqrt(sums / model_width + EPSILON)
    logits = lax.dot_general(final, head, (((1,), (1,)), ((), ())), preferred_element_type=F32)
    logits = logits * final_scale[:, None]

    source_of = jnp.arange(row_total, dtype=jnp.int32) % SOURCES
    parent_row = parents[0] * SOURCES + source_of
    vocab_offset = lax.axis_index(("section", "dp", "vocab")) * vocab_rows
    parent_logits = jnp.take(logits, parent_row, axis=0)
    is_pick = jnp.arange(vocab_rows, dtype=jnp.int32)[None, :] + vocab_offset == picks[0][:, None]
    picked = jnp.sum(jnp.where(is_pick, parent_logits, 0.0), axis=1)
    top = jnp.max(logits, axis=1)
    total = jnp.sum(jnp.exp(logits - top[:, None]), axis=1)
    for axes in (("dp", "vocab"), ("section",)):
        stats = jnp.stack([top, total, picked] + [jnp.zeros_like(top)] * 5)
        stats = jnp.pad(stats, ((0, 0), (0, 128 - row_total)))
        copies = jnp.broadcast_to(stats[None], (lax.axis_size(axes),) + stats.shape)
        every = lax.all_to_all(copies, axes, 0, 0, tiled=True)[:, :, :row_total]
        tops, totals, picks_of = every[:, 0], every[:, 1], every[:, 2]
        top = jnp.max(tops, axis=0)
        total = jnp.sum(totals * jnp.exp(tops - top[None]), axis=0)
        picked = jnp.sum(picks_of, axis=0)
    log_norm = top + jnp.log(total)
    scores_now = jnp.take(scores, parent_row) + picked - jnp.take(log_norm, parent_row)

    conv_next = jnp.concatenate([conv_old[:, 1:], x_kept[:, None]], axis=1)
    states = jnp.concatenate([ssm_now.astype(BF16), conv_next], axis=1)
    every = lax.all_gather(states, "dp", axis=0, tiled=False)
    beams = lax.dynamic_slice_in_dim(parents[0], dp_at * own_rows, own_rows, 0)
    mine = jnp.stack(
        [
            lax.dynamic_index_in_dim(every[:, r], beams[r], 0, keepdims=False)
            for r in range(own_rows)
        ]
    )
    ssm_new = mine[:, :STATE_DIM].astype(F32)
    return (mine[:, STATE_DIM:][None], ssm_new[None], scores_now)


def solution(mesh):
    placed = (
        P(),
        P(),
        P(),
        P(),
        P("section", ("dp", "vocab")),
        P("section", ("dp", "vocab")),
        P("section", ("dp", "vocab"), None, None),
        P("section", None, "vocab"),
        P("section", "vocab"),
        P("section", "vocab", None),
        P("section", "vocab", None),
        P("section", None, "vocab"),
        P("section", "vocab"),
        P("section", None, "vocab"),
        P("section", "vocab"),
        P("section", None, ("dp", "vocab")),
        P(),
        P(("section", "dp", "vocab"), None),
        P("section", "dp", None, "vocab"),
        P("section", "dp", None, "vocab"),
    )
    return jax.shard_map(
        on_device,
        mesh=mesh,
        in_specs=placed,
        out_specs=(P("section", "dp", None, "vocab"), P("section", "dp", None, "vocab"), P()),
        check_vma=False,
    )
```

```python
import jax
import jax.numpy as jnp
from jax import lax
from jax.experimental import pallas as pl
from jax.experimental.pallas import tpu as pltpu
from jax.sharding import PartitionSpec as P

STATE_DIM = 16
SOURCES = 4
EPSILON = 1e-05
TAIL = 128
PAD = 8

F32 = jnp.float32
BF16 = jnp.bfloat16


def by_vocab(value, by):
    n = lax.axis_size("vocab")
    return lax.ppermute(value, "vocab", [(i, (i + by) % n) for i in range(n)])


def by_y(value, by):
    n = lax.axis_size("dp") // 2
    pairs = [(2 * y + c, 2 * ((y + by) % n) + c) for y in range(n) for c in range(2)]
    return lax.ppermute(value, "dp", pairs)


def other_core(value):
    n = lax.axis_size("dp")
    return lax.ppermute(value, "dp", [(i, i ^ 1) for i in range(n)])


def next_section(value, y_by=0):
    sections = lax.axis_size("section")
    dp = lax.axis_size("dp")
    n = dp // 2
    pairs = [
        (s * dp + 2 * y + c, ((s + 1) % sections) * dp + 2 * ((y + y_by) % n) + c)
        for s in range(sections)
        for y in range(n)
        for c in range(2)
    ]
    return lax.ppermute(value, ("section", "dp"), pairs)


def whole(space=pltpu.VMEM):
    return pl.BlockSpec(memory_space=space)


def pack_blocks(at_ref, i0, i1, i2, i3, o0, o1, o2, o3):
    for i_ref, o_ref in ((i0, o0), (i1, o1), (i2, o2), (i3, o3)):
        o_ref[...] = i_ref[...]


def place_rows(groups, own_rows, at_ref, b0, b1, b2, b3, hidden_ref, gain_ref):
    y, c, v = at_ref[0], at_ref[1], at_ref[2]
    block = b0.shape[2]
    stride = b0.shape[0] // 2
    core_width = 4 * block
    for k, ref in enumerate((b0, b1, b2, b3)):
        for half in range(2):
            at = pl.multiple_of(lax.rem(v + 4 - k, 4) * block + half * core_width, block)
            columns = pl.ds(at, block)
            gain_ref[:, columns] = ref[half * stride + groups, 0:1, :]
            for j in range(4):
                group = 2 * lax.rem(y + j, 4) + c + half * stride
                there = slice(j * own_rows, (j + 1) * own_rows)
                hidden_ref[there, columns] = ref[group]


def project_in(
    columns, at_ref, p_ref, d0, d1, d2, d3, gain_ref, w0, w1, w2, w3, x0, x1, x2, x3,
    o0, o1, o2, o3, hidden_ref, normed, scr,
):
    block, wide = w0.shape
    rows = o0.shape[0]
    outs = (o0, o1, o2, o3)
    added = d0[...].astype(F32) + d1[...].astype(F32) + d2[...].astype(F32) + d3[...].astype(F32)
    hidden = p_ref[...] + added
    hidden_ref[...] = hidden
    normed[...] = hidden * gain_ref[...]
    squares = jnp.sum(hidden * hidden, axis=1, keepdims=True)
    high = squares.astype(BF16).astype(F32)
    lane = lax.broadcasted_iota(jnp.int32, (hidden.shape[0], TAIL), 1)
    scr[:, wide:] = jnp.where(lane == 0, high, jnp.where(lane == 1, squares - high, 0.0))
    lefts = []
    for half in range(2):
        for k in range(4):
            at = lax.rem(at_ref[2] + 4 - k, 4) * block + half * 4 * block
            lefts.append(normed[:, pl.ds(pl.multiple_of(at, block), block)].astype(BF16))
    for at in range(0, wide, columns):
        part = jnp.zeros((hidden.shape[0], columns), F32)
        for left, w in zip(lefts, (w0, w1, w2, w3, x0, x1, x2, x3)):
            part = part + jnp.dot(left, w[:, at : at + columns], preferred_element_type=F32)
        scr[:, at : at + columns] = part
    for k, out in enumerate(outs):
        out[...] = scr[k * rows : (k + 1) * rows, :].astype(BF16)


def convolve(model_width, a0, a1, a2, a3, small_ref, w_x, part_ref, side_ref):
    total = (
        a0[...].astype(F32) + a1[...].astype(F32) + a2[...].astype(F32) + a3[...].astype(F32)
    )
    rows = total.shape[0]
    wide = total.shape[1] - TAIL
    half = wide // 2
    squares = total[:, wide : wide + 1] + total[:, wide + 1 : wide + 2]
    scale = lax.rsqrt(squares / model_width + EPSILON)
    projected = (total[:, :wide] * scale).astype(BF16).astype(F32)
    x = projected[:, :half]
    z = projected[:, half:]
    act = jax.nn.silu(small_ref[0:rows, :] + x * small_ref[rows : rows + 1, :])
    part_ref[...] = jnp.dot(act.astype(BF16), w_x[...], preferred_element_type=F32)
    side_ref[0] = act
    side_ref[1] = jax.nn.silu(z)
    side_ref[2] = x


def advance(
    section, at_ref, p0, p1, p2, p3, side_ref, w_dt, small_ref, x_in, ssm_in,
    mixed_ref, x_out, ssm_out, scr,
):
    terms = p0[...] + p1[...] + p2[...] + p3[...]
    rank = w_dt.shape[0]
    rows = terms.shape[0]
    low = terms[:, :rank].astype(BF16)
    pre = jnp.dot(low, w_dt[...], preferred_element_type=F32)
    pre = pre + small_ref[rows + 1 : rows + 2, :]
    step = jnp.maximum(pre, 0.0) + jnp.log1p(jnp.exp(-jnp.abs(pre)))
    act = side_ref[0]
    scr[0] = step
    scr[1] = step * act
    bc = terms[:, rank : rank + 2 * STATE_DIM]
    shape = (STATE_DIM, 2 * STATE_DIM)
    lane = lax.broadcasted_iota(jnp.int32, shape, 1)
    sub = lax.broadcasted_iota(jnp.int32, shape, 0)
    rates = small_ref[PAD:, :]
    live = at_ref[3] == section
    for g in range(rows):
        line = jnp.broadcast_to(bc[g : g + 1, :], shape)
        b_col = jnp.sum(jnp.where(lane == sub, line, 0.0), axis=1, keepdims=True)
        c_col = jnp.sum(jnp.where(lane == sub + STATE_DIM, line, 0.0), axis=1, keepdims=True)
        old = ssm_in[g]
        new = jnp.exp(-scr[0, g : g + 1, :] * rates) * old + b_col * scr[1, g : g + 1, :]
        scr[2, g : g + 1, :] = jnp.sum(c_col * new, axis=0, keepdims=True)
        ssm_out[g] = jnp.where(live, new, old)
    x_out[...] = jnp.where(live, side_ref[2], x_in[...])
    mixed = (scr[2] + small_ref[rows + 2 : rows + 3, :] * act) * side_ref[1]
    mixed_ref[...] = mixed.astype(BF16)


def project_out(
    at_ref, m0, m1, m2, m3, w0, w1, w2, w3, x0, x1, x2, x3, out_ref, scr
):
    rows = m0.shape[0]
    block = w0.shape[1]
    for k, ref in enumerate((m0, m1, m2, m3)):
        scr[k * rows : (k + 1) * rows, :] = ref[...].astype(F32)
    mixed = scr[...].astype(BF16)
    for half, blocks in enumerate(((w0, w1, w2, w3), (x0, x1, x2, x3))):
        for k, w in enumerate(blocks):
            at = lax.rem(at_ref[2] + 4 - k, 4) * block + half * 4 * block
            part = jnp.dot(mixed, w[...], preferred_element_type=F32)
            out_ref[:, pl.ds(pl.multiple_of(at, block), block)] = part.astype(BF16)


def finish(own_rows, at_ref, p_ref, d0, d1, d2, d3, gain_ref, out_ref, scr, turned):
    added = d0[...].astype(F32) + d1[...].astype(F32) + d2[...].astype(F32) + d3[...].astype(F32)
    turned[...] = p_ref[...] + added
    for k in range(4):
        scr[k] = turned[k * own_rows : (k + 1) * own_rows, :]
    for y in range(4):
        turned[y * own_rows : (y + 1) * own_rows, :] = scr[lax.rem(y + 4 - at_ref[0], 4)]
    rows = turned[...]
    width = rows.shape[1]
    half = width // 2
    first = at_ref[1] == 0
    left = jnp.where(first, rows[:, :half], rows[:, half:])
    right = jnp.where(first, rows[:, half:], rows[:, :half])
    out_ref[:, :half] = (left * gain_ref[:, :half]).astype(BF16)
    out_ref[:, half:width] = (right * gain_ref[:, half:]).astype(BF16)
    squares = jnp.sum(rows * rows, axis=1, keepdims=True)
    high = squares.astype(BF16).astype(F32)
    lane = lax.broadcasted_iota(jnp.int32, (rows.shape[0], TAIL), 1)
    tail = jnp.where(lane == 0, high, jnp.where(lane == 1, squares - high, 0.0))
    out_ref[:, width:] = tail.astype(BF16)


def local_call(body, outs, scratch=(), smem=0, operands=0, aliases=None, cost=None):
    specs = [whole(pltpu.SMEM)] * smem + [whole()] * (operands - smem)
    return pl.pallas_call(
        body,
        out_shape=[jax.ShapeDtypeStruct(shape, dtype) for shape, dtype in outs],
        in_specs=specs,
        out_specs=[whole()] * len(outs),
        scratch_shapes=[pltpu.VMEM(shape, F32) for shape in scratch],
        input_output_aliases=aliases or {},
        compiler_params=pltpu.CompilerParams(vmem_limit_bytes=12 * 2**20),
        cost_estimate=cost,
    )


def on_device(
    tokens_in,
    picks,
    parents,
    scores,
    embed,
    norm_gain,
    in_weight,
    conv_weight,
    conv_bias,
    xdt_weight,
    xbc_weight,
    dt_weight,
    dt_bias,
    a_rate,
    skip,
    out_weight,
    final_gain,
    head,
    conv_state,
    ssm_state,
):
    section_count = lax.axis_size("section")
    dp_count = lax.axis_size("dp")
    vocab_count = lax.axis_size("vocab")
    y_count = dp_count // 2
    row_total = tokens_in.shape[0]
    own_rows = row_total // dp_count
    core_rows = own_rows * y_count
    section_at = lax.axis_index("section")
    dp_at = lax.axis_index("dp")
    vocab_at = lax.axis_index("vocab")
    y_at = dp_at // 2
    core_at = dp_at % 2
    block = in_weight.shape[1]
    chan = in_weight.shape[3] // vocab_count
    model_width = final_gain.shape[0]
    core_width = block * vocab_count
    y_width = 2 * core_width
    vocab_rows = head.shape[0]

    coords = jnp.stack([y_at, core_at, vocab_at, section_at]).astype(jnp.int32)

    w_in = lax.optimization_barrier(in_weight[0].reshape(block, 2 * vocab_count * chan))
    in_blocks = pl.pallas_call(
        pack_blocks,
        out_shape=[jax.ShapeDtypeStruct((block, 2 * chan), BF16)] * vocab_count,
        grid_spec=pltpu.PrefetchScalarGridSpec(
            num_scalar_prefetch=1,
            grid=(2,),
            in_specs=[
                pl.BlockSpec(
                    (block, chan),
                    lambda i, at, k=k: (0, i * vocab_count + lax.rem(at[2] + k, vocab_count)),
                )
                for k in range(vocab_count)
            ],
            out_specs=[pl.BlockSpec((block, chan), lambda i, at: (0, i))] * vocab_count,
        ),
    )(coords, *([w_in] * vocab_count))
    in_blocks = list(in_blocks)
    in_blocks = in_blocks[:1] + [by_vocab(in_blocks[k], k) for k in range(1, vocab_count)]

    embed_rows = embed.shape[0]
    local_ids = tokens_in - section_at * embed_rows
    inside = (local_ids >= 0) & (local_ids < embed_rows)
    found = jnp.take(embed, jnp.clip(local_ids, 0, embed_rows - 1), axis=0)
    found = jnp.where(inside[:, None], found, 0).astype(BF16)
    span = section_count // 2
    while span:
        pairs = [(i + span, i) for i in range(span)]
        found = found + lax.ppermute(found, "section", pairs)
        span //= 2
    looked_up = found.astype(F32).reshape(dp_count, own_rows, block)
    beside = jnp.pad(norm_gain, ((0, own_rows - 1), (0, 0)))
    bundle = jnp.concatenate([looked_up, beside[None]], axis=0)
    bundle = jnp.concatenate([bundle, other_core(bundle)], axis=0)
    _, w_out = lax.optimization_barrier((bundle, out_weight[0]))
    bundles = [bundle] + [by_vocab(bundle, k) for k in range(1, vocab_count)]
    hidden, gain = local_call(
        lambda *refs: place_rows(dp_count, own_rows, *refs),
        [((core_rows, y_width), F32), ((1, y_width), F32)],
        smem=1,
        operands=5,
    )(coords, *bundles)

    w_out = next_section(w_out)
    in_blocks = in_blocks + [other_core(piece) for piece in in_blocks]

    def exchange_out(w_out):
        w_out = w_out.reshape(vocab_count, chan, block)
        blocks = [
            lax.dynamic_index_in_dim(w_out, (vocab_at + k) % vocab_count, 0, keepdims=False)
            for k in range(vocab_count)
        ]
        return blocks[:1] + [by_vocab(blocks[k], k) for k in range(1, vocab_count)]

    w_x = jnp.concatenate([xdt_weight[0], xbc_weight[0]], axis=1)
    w_dt = dt_weight[0]
    taps = conv_weight[0]
    conv_old = conv_state[0]
    keep = taps.shape[0] - 1
    conv_pre = conv_bias + jnp.sum(conv_old.astype(F32) * taps[None, :keep], axis=1)
    small = jnp.concatenate(
        [conv_pre, taps[keep:], dt_bias, skip, jnp.zeros((1, chan), F32), a_rate[0]], axis=0
    )
    ssm_now = ssm_state[0]
    x_kept = jnp.zeros((own_rows, chan), F32)

    wide = 2 * chan + TAIL
    terms_wide = w_x.shape[1]
    call_in = local_call(
        lambda *refs: project_in(512, *refs),
        [((own_rows, wide), BF16)] * y_count + [((core_rows, y_width), F32)],
        scratch=[(core_rows, y_width), (core_rows, wide)],
        smem=1,
        operands=7 + 2 * vocab_count,
        cost=pl.CostEstimate(
            flops=4 * core_rows * y_width * chan, bytes_accessed=4 * y_width * chan, transcendentals=0
        ),
    )
    call_conv = local_call(
        lambda *refs: convolve(model_width, *refs),
        [((own_rows, terms_wide), F32), ((3, own_rows, chan), F32)],
        operands=6,
        cost=pl.CostEstimate(
            flops=2 * own_rows * chan * terms_wide,
            bytes_accessed=2 * chan * terms_wide,
            transcendentals=2 * own_rows * chan,
        ),
    )
    def call_state(section, *operands):
        return local_call(
            lambda *refs: advance(section, *refs),
            [((own_rows, chan), BF16), ((own_rows, chan), F32), (ssm_now.shape, F32)],
            scratch=[(3, own_rows, chan)],
            smem=1,
            operands=10,
            aliases={8: 1, 9: 2},
            cost=pl.CostEstimate(
                flops=2 * own_rows * chan * dt_weight.shape[1],
                bytes_accessed=2 * chan * dt_weight.shape[1] + 8 * ssm_now.size,
                transcendentals=ssm_now.size,
            ),
        )(*operands)

    call_out = local_call(
        project_out,
        [((core_rows, y_width), BF16)],
        scratch=[(core_rows, chan)],
        smem=1,
        operands=5 + 2 * vocab_count,
        cost=pl.CostEstimate(
            flops=2 * core_rows * y_width * chan, bytes_accessed=2 * y_width * chan, transcendentals=0
        ),
    )

    adds = [jnp.zeros((core_rows, y_width), BF16)] * vocab_count
    for step in range(section_count):
        *parts, hidden = call_in(coords, hidden, *adds, gain, *in_blocks)
        if step == 0:
            _, w_out = lax.optimization_barrier((hidden, w_out))
            out_blocks = exchange_out(w_out)
        hidden = next_section(hidden)
        parts = parts[:1] + [by_y(parts[k], k) for k in range(1, y_count)]
        terms, side = call_conv(*parts, small, w_x)
        all_terms = [terms] + [by_vocab(terms, k) for k in range(1, vocab_count)]
        mixed, x_kept, ssm_now = call_state(
            step, coords, *all_terms, side, w_dt, small, x_kept, ssm_now
        )
        if step == 0:
            _, out_blocks = lax.optimization_barrier((mixed, out_blocks))
            out_blocks = out_blocks + [other_core(piece) for piece in out_blocks]
        mixes = [next_section(mixed, -k) for k in range(y_count)]
        (added,) = call_out(coords, *mixes, *out_blocks)
        adds = [added] + [by_vocab(added, k) for k in range(1, vocab_count)]

    y_gain = lax.dynamic_slice_in_dim(final_gain, y_at * y_width, y_width, 0)
    (sent,) = local_call(
        lambda *refs: finish(own_rows, *refs),
        [((core_rows, y_width + TAIL), BF16)],
        scratch=[(y_count, own_rows, y_width), (core_rows, y_width)],
        smem=1,
        operands=7,
    )(coords, hidden, *adds, y_gain[None])
    middle = section_count // 2
    got = lax.ppermute(sent, "section", [(0, middle)])
    sent = jnp.where(section_at == middle, got, sent)
    received = jnp.zeros_like(sent)
    for k in range(1, middle):
        pairs = [(0, k), (middle, middle + k)]
        received = received + lax.ppermute(sent, "section", pairs)
    is_source = (section_at == middle) | (section_at == 0)
    sent = jnp.where(is_source, sent, received)
    every_y = jnp.stack([sent] + [by_y(sent, -k) for k in range(1, y_count)])
    every_y = jnp.roll(every_y, y_at, axis=0)
    facing = other_core(every_y)
    cores = jnp.where(core_at == 0, jnp.stack([every_y, facing]), jnp.stack([facing, every_y]))
    cores = cores.reshape(2, y_count, y_count, own_rows, y_width + TAIL)
    cores = jnp.transpose(cores, (2, 0, 3, 1, 4))
    sums = jnp.sum(cores[..., y_width : y_width + 2].astype(F32), axis=(3, 4)).reshape(row_total)
    final = cores[..., :y_width].reshape(row_total, model_width)
    final_scale = lax.rsqrt(sums / model_width + EPSILON)
    logits = lax.dot_general(final, head, (((1,), (1,)), ((), ())), preferred_element_type=F32)
    logits = logits * final_scale[:, None]

    source_of = jnp.arange(row_total, dtype=jnp.int32) % SOURCES
    parent_row = parents[0] * SOURCES + source_of
    vocab_offset = lax.axis_index(("section", "dp", "vocab")) * vocab_rows
    parent_logits = jnp.take(logits, parent_row, axis=0)
    is_pick = jnp.arange(vocab_rows, dtype=jnp.int32)[None, :] + vocab_offset == picks[0][:, None]
    picked = jnp.sum(jnp.where(is_pick, parent_logits, 0.0), axis=1)
    top = jnp.max(logits, axis=1)
    total = jnp.sum(jnp.exp(logits - top[:, None]), axis=1)
    for axes in (("dp", "vocab"), ("section",)):
        stats = jnp.stack([top, total, picked] + [jnp.zeros_like(top)] * 5)
        stats = jnp.pad(stats, ((0, 0), (0, 128 - row_total)))
        copies = jnp.broadcast_to(stats[None], (lax.axis_size(axes),) + stats.shape)
        every = lax.all_to_all(copies, axes, 0, 0, tiled=True)[:, :, :row_total]
        tops, totals, picks_of = every[:, 0], every[:, 1], every[:, 2]
        top = jnp.max(tops, axis=0)
        total = jnp.sum(totals * jnp.exp(tops - top[None]), axis=0)
        picked = jnp.sum(picks_of, axis=0)
    log_norm = top + jnp.log(total)
    scores_now = jnp.take(scores, parent_row) + picked - jnp.take(log_norm, parent_row)

    conv_next = jnp.concatenate([conv_old[:, 1:], x_kept.astype(BF16)[:, None]], axis=1)
    states = jnp.concatenate([ssm_now.astype(BF16), conv_next], axis=1)
    every = lax.all_gather(states, "dp", axis=0, tiled=False)
    beams = lax.dynamic_slice_in_dim(parents[0], dp_at * own_rows, own_rows, 0)
    mine = jnp.stack(
        [
            lax.dynamic_index_in_dim(every[:, r], beams[r], 0, keepdims=False)
            for r in range(own_rows)
        ]
    )
    ssm_new = mine[:, :STATE_DIM].astype(F32)
    return (mine[:, STATE_DIM:][None], ssm_new[None], scores_now)


def solution(mesh):
    placed = (
        P(),
        P(),
        P(),
        P(),
        P("section", ("dp", "vocab")),
        P("section", ("dp", "vocab")),
        P("section", ("dp", "vocab"), None, None),
        P("section", None, "vocab"),
        P("section", "vocab"),
        P("section", "vocab", None),
        P("section", "vocab", None),
        P("section", None, "vocab"),
        P("section", "vocab"),
        P("section", None, "vocab"),
        P("section", "vocab"),
        P("section", None, ("dp", "vocab")),
        P(),
        P(("section", "dp", "vocab"), None),
        P("section", "dp", None, "vocab"),
        P("section", "dp", None, "vocab"),
    )
    return jax.shard_map(
        on_device,
        mesh=mesh,
        in_specs=placed,
        out_specs=(P("section", "dp", None, "vocab"), P("section", "dp", None, "vocab"), P()),
        check_vma=False,
    )
```

```python
import jax
import jax.numpy as jnp
from jax import lax
from jax.experimental import pallas as pl
from jax.experimental.pallas import tpu as pltpu
from jax.sharding import PartitionSpec as P

STATE_DIM = 16
SOURCES = 4
EPSILON = 1e-05
TAIL = 128
PAD = 8

F32 = jnp.float32
BF16 = jnp.bfloat16


def by_vocab(value, by):
    n = lax.axis_size("vocab")
    return lax.ppermute(value, "vocab", [(i, (i + by) % n) for i in range(n)])


def over_side(value):
    n = lax.axis_size("dp") // 2
    m = lax.axis_size("vocab")
    groups = [[(2 * y + c) * m + v for y in range(n) for v in range(m)] for c in range(2)]
    return lax.all_to_all(value, ("dp", "vocab"), 0, 0, tiled=True, axis_index_groups=groups)


def other_core(value):
    n = lax.axis_size("dp")
    return lax.ppermute(value, "dp", [(i, i ^ 1) for i in range(n)])


def next_section(value):
    n = lax.axis_size("section")
    return lax.ppermute(value, "section", [(i, (i + 1) % n) for i in range(n)])


def whole(space=pltpu.VMEM):
    return pl.BlockSpec(memory_space=space)


def place_rows(groups, at_ref, own_ref, oth_ref, hidden_ref, gain_ref):
    rows, block = own_ref.shape[1:]
    for half, ref in enumerate((own_ref, oth_ref)):
        columns = slice(half * block, (half + 1) * block)
        gain_ref[:, columns] = ref[groups, 0:1, :]
        for y in range(groups // 2):
            hidden_ref[y * rows : (y + 1) * rows, columns] = ref[2 * y + at_ref[1]]


def project_in(columns, h_ref, gain_ref, w_own, w_oth, out_ref, scr):
    block, wide = w_own.shape
    rows = out_ref.shape[1]
    chan = (out_ref.shape[2] - TAIL) // 2
    sides = wide // (2 * chan)
    hidden = h_ref[...]
    normed = (hidden * gain_ref[...]).astype(BF16)
    squares = jnp.sum(hidden * hidden, axis=1, keepdims=True)
    high = squares.astype(BF16).astype(F32)
    lane = lax.broadcasted_iota(jnp.int32, (hidden.shape[0], TAIL), 1)
    scr[:, wide:] = jnp.where(lane == 0, high, jnp.where(lane == 1, squares - high, 0.0))
    for at in range(0, wide, columns):
        there = slice(at, at + columns)
        part = jnp.dot(normed[:, :block], w_own[:, there], preferred_element_type=F32)
        part = part + jnp.dot(normed[:, block:], w_oth[:, there], preferred_element_type=F32)
        scr[:, there] = part
    for y in range(out_ref.shape[0] // sides):
        own = slice(y * rows, (y + 1) * rows)
        for v in range(sides):
            for half in range(2):
                at = (half * sides + v) * chan
                out_ref[y * sides + v, :, half * chan : (half + 1) * chan] = scr[
                    own, at : at + chan
                ].astype(BF16)
            out_ref[y * sides + v, :, 2 * chan :] = scr[own, wide:].astype(BF16)


def convolve(model_width, sums_ref, small_ref, w_x, part_ref, side_ref):
    total = sums_ref[0].astype(F32)
    for i in range(1, sums_ref.shape[0]):
        total = total + sums_ref[i].astype(F32)
    rows = total.shape[0]
    wide = total.shape[1] - TAIL
    half = wide // 2
    squares = total[:, wide : wide + 1] + total[:, wide + 1 : wide + 2]
    scale = lax.rsqrt(squares / model_width + EPSILON)
    projected = (total[:, :wide] * scale).astype(BF16).astype(F32)
    x = projected[:, :half]
    z = projected[:, half:]
    act = jax.nn.silu(small_ref[0:rows, :] + x * small_ref[rows : rows + 1, :])
    part_ref[...] = jnp.dot(act.astype(BF16), w_x[...], preferred_element_type=F32)
    side_ref[0] = act
    side_ref[1] = jax.nn.silu(z)
    side_ref[2] = x


def advance(
    section, at_ref, p0, p1, p2, p3, side_ref, w_dt, small_ref, x_in, ssm_in,
    mixed_ref, x_out, ssm_out, scr,
):
    terms = p0[...] + p1[...] + p2[...] + p3[...]
    rank = w_dt.shape[0]
    rows = terms.shape[0]
    low = terms[:, :rank].astype(BF16)
    pre = jnp.dot(low, w_dt[...], preferred_element_type=F32)
    pre = pre + small_ref[rows + 1 : rows + 2, :]
    step = jnp.maximum(pre, 0.0) + jnp.log1p(jnp.exp(-jnp.abs(pre)))
    act = side_ref[0]
    scr[0] = step
    scr[1] = step * act
    bc = terms[:, rank : rank + 2 * STATE_DIM]
    shape = (STATE_DIM, 2 * STATE_DIM)
    lane = lax.broadcasted_iota(jnp.int32, shape, 1)
    sub = lax.broadcasted_iota(jnp.int32, shape, 0)
    rates = small_ref[PAD:, :]
    live = at_ref[3] == section
    for g in range(rows):
        line = jnp.broadcast_to(bc[g : g + 1, :], shape)
        b_col = jnp.sum(jnp.where(lane == sub, line, 0.0), axis=1, keepdims=True)
        c_col = jnp.sum(jnp.where(lane == sub + STATE_DIM, line, 0.0), axis=1, keepdims=True)
        old = ssm_in[g]
        new = jnp.exp(-scr[0, g : g + 1, :] * rates) * old + b_col * scr[1, g : g + 1, :]
        scr[2, g : g + 1, :] = jnp.sum(c_col * new, axis=0, keepdims=True)
        ssm_out[g] = jnp.where(live, new, old)
    x_out[...] = jnp.where(live, side_ref[2], x_in[...])
    mixed = (scr[2] + small_ref[rows + 2 : rows + 3, :] * act) * side_ref[1]
    mixed = mixed.astype(BF16)
    for i in range(mixed_ref.shape[0]):
        mixed_ref[i] = mixed


def project_out(sides, m_ref, h_ref, w_ref, out_ref, scr):
    rows, chan = m_ref.shape[1:]
    total = h_ref[...]
    for v in range(sides):
        for y in range(m_ref.shape[0] // sides):
            scr[y * rows : (y + 1) * rows, :] = m_ref[y * sides + v].astype(F32)
        total = total + jnp.dot(
            scr[...].astype(BF16),
            w_ref[v * chan : (v + 1) * chan, :],
            preferred_element_type=F32,
        )
    out_ref[...] = total


def finish(at_ref, h_ref, gain_ref, out_ref):
    rows = h_ref[...]
    width = rows.shape[1]
    half = width // 2
    first = at_ref[1] == 0
    left = jnp.where(first, rows[:, :half], rows[:, half:])
    right = jnp.where(first, rows[:, half:], rows[:, :half])
    out_ref[:, :half] = (left * gain_ref[:, :half]).astype(BF16)
    out_ref[:, half:width] = (right * gain_ref[:, half:]).astype(BF16)
    squares = jnp.sum(rows * rows, axis=1, keepdims=True)
    high = squares.astype(BF16).astype(F32)
    lane = lax.broadcasted_iota(jnp.int32, (rows.shape[0], TAIL), 1)
    tail = jnp.where(lane == 0, high, jnp.where(lane == 1, squares - high, 0.0))
    out_ref[:, width:] = tail.astype(BF16)


def local_call(body, outs, scratch=(), smem=0, operands=0, aliases=None, cost=None):
    specs = [whole(pltpu.SMEM)] * smem + [whole()] * (operands - smem)
    return pl.pallas_call(
        body,
        out_shape=[jax.ShapeDtypeStruct(shape, dtype) for shape, dtype in outs],
        in_specs=specs,
        out_specs=[whole()] * len(outs),
        scratch_shapes=[pltpu.VMEM(shape, F32) for shape in scratch],
        input_output_aliases=aliases or {},
        compiler_params=pltpu.CompilerParams(vmem_limit_bytes=12 * 2**20),
        cost_estimate=cost,
    )


def on_device(
    tokens_in,
    picks,
    parents,
    scores,
    embed,
    norm_gain,
    in_weight,
    conv_weight,
    conv_bias,
    xdt_weight,
    xbc_weight,
    dt_weight,
    dt_bias,
    a_rate,
    skip,
    out_weight,
    final_gain,
    head,
    conv_state,
    ssm_state,
):
    section_count = lax.axis_size("section")
    dp_count = lax.axis_size("dp")
    vocab_count = lax.axis_size("vocab")
    y_count = dp_count // 2
    row_total = tokens_in.shape[0]
    own_rows = row_total // dp_count
    core_rows = own_rows * y_count
    section_at = lax.axis_index("section")
    dp_at = lax.axis_index("dp")
    vocab_at = lax.axis_index("vocab")
    y_at = dp_at // 2
    core_at = dp_at % 2
    block = in_weight.shape[1]
    chan = in_weight.shape[3] // vocab_count
    model_width = final_gain.shape[0]
    pair_width = 2 * block
    sides = y_count * vocab_count
    vocab_rows = head.shape[0]

    coords = jnp.stack([y_at, core_at, vocab_at, section_at]).astype(jnp.int32)

    in_own = in_weight[0].reshape(block, 2 * vocab_count * chan)
    in_oth = other_core(in_own)
    w_out = jnp.concatenate([out_weight[0], other_core(out_weight[0])], axis=1)

    embed_rows = embed.shape[0]
    local_ids = tokens_in - section_at * embed_rows
    inside = (local_ids >= 0) & (local_ids < embed_rows)
    found = jnp.take(embed, jnp.clip(local_ids, 0, embed_rows - 1), axis=0)
    found = jnp.where(inside[:, None], found, 0).astype(BF16)
    span = section_count // 2
    while span:
        pairs = [(i + span, i) for i in range(span)]
        found = found + lax.ppermute(found, "section", pairs)
        span //= 2
    looked_up = found.astype(F32).reshape(dp_count, own_rows, block)
    beside = jnp.pad(norm_gain, ((0, own_rows - 1), (0, 0)))
    bundle = jnp.concatenate([looked_up, beside[None]], axis=0)
    hidden, gain = local_call(
        lambda *refs: place_rows(dp_count, *refs),
        [((core_rows, pair_width), F32), ((1, pair_width), F32)],
        smem=1,
        operands=3,
    )(coords, bundle, other_core(bundle))

    w_x = jnp.concatenate([xdt_weight[0], xbc_weight[0]], axis=1)
    w_dt = dt_weight[0]
    taps = conv_weight[0]
    conv_old = conv_state[0]
    keep = taps.shape[0] - 1
    conv_pre = conv_bias + jnp.sum(conv_old.astype(F32) * taps[None, :keep], axis=1)
    small = jnp.concatenate(
        [conv_pre, taps[keep:], dt_bias, skip, jnp.zeros((1, chan), F32), a_rate[0]], axis=0
    )
    ssm_now = ssm_state[0]
    x_kept = jnp.zeros((own_rows, chan), F32)

    wide = 2 * chan + TAIL
    terms_wide = w_x.shape[1]
    call_in = local_call(
        lambda *refs: project_in(512, *refs),
        [((sides, own_rows, wide), BF16)],
        scratch=[(core_rows, 2 * vocab_count * chan + TAIL)],
        operands=4,
        cost=pl.CostEstimate(
            flops=4 * core_rows * pair_width * vocab_count * chan,
            bytes_accessed=4 * pair_width * vocab_count * chan,
            transcendentals=0,
        ),
    )
    call_conv = local_call(
        lambda *refs: convolve(model_width, *refs),
        [((own_rows, terms_wide), F32), ((3, own_rows, chan), F32)],
        operands=3,
        cost=pl.CostEstimate(
            flops=2 * own_rows * chan * terms_wide,
            bytes_accessed=2 * chan * terms_wide,
            transcendentals=2 * own_rows * chan,
        ),
    )
    def call_state(section, *operands):
        return local_call(
            lambda *refs: advance(section, *refs),
            [((sides, own_rows, chan), BF16), ((own_rows, chan), F32), (ssm_now.shape, F32)],
            scratch=[(3, own_rows, chan)],
            smem=1,
            operands=10,
            aliases={8: 1, 9: 2},
            cost=pl.CostEstimate(
                flops=2 * own_rows * chan * dt_weight.shape[1],
                bytes_accessed=2 * chan * dt_weight.shape[1] + 8 * ssm_now.size,
                transcendentals=ssm_now.size,
            ),
        )(*operands)

    call_out = local_call(
        lambda *refs: project_out(vocab_count, *refs),
        [((core_rows, pair_width), F32)],
        scratch=[(core_rows, chan)],
        operands=3,
        cost=pl.CostEstimate(
            flops=2 * core_rows * pair_width * vocab_count * chan,
            bytes_accessed=2 * pair_width * vocab_count * chan,
            transcendentals=0,
        ),
    )

    for step in range(section_count):
        (parts,) = call_in(hidden, gain, in_own, in_oth)
        terms, side = call_conv(over_side(parts), small, w_x)
        all_terms = [terms] + [by_vocab(terms, k) for k in range(1, vocab_count)]
        mixed, x_kept, ssm_now = call_state(
            step, coords, *all_terms, side, w_dt, small, x_kept, ssm_now
        )
        (hidden,) = call_out(over_side(mixed), hidden, w_out)
        if step + 1 < section_count:
            hidden = next_section(hidden)

    pair_gain = final_gain.reshape(y_count, 2, vocab_count, block)
    pair_gain = lax.dynamic_index_in_dim(pair_gain, y_at, 0, keepdims=False)
    pair_gain = lax.dynamic_index_in_dim(pair_gain, vocab_at, 1, keepdims=False)
    (sent,) = local_call(
        finish,
        [((core_rows, pair_width + TAIL), BF16)],
        smem=1,
        operands=3,
    )(coords, hidden, pair_gain.reshape(1, pair_width))
    last = section_count - 1
    middle = last // 2
    got = lax.ppermute(sent, "section", [(last, middle)])
    sent = jnp.where(section_at == middle, got, sent)
    received = jnp.zeros_like(sent)
    for k in range(1, middle + 1):
        pairs = [(last, (last + k) % section_count), (middle, middle + k)]
        received = received + lax.ppermute(sent, "section", pairs)
    is_source = (section_at == middle) | (section_at == last)
    sent = jnp.where(is_source, sent, received)
    every = over_side(jnp.broadcast_to(sent[None], (sides,) + sent.shape))
    facing = other_core(every)
    cores = jnp.where(core_at == 0, jnp.stack([every, facing]), jnp.stack([facing, every]))
    cores = cores.reshape(2, y_count, vocab_count, y_count, own_rows, pair_width + TAIL)
    sums = jnp.sum(cores[..., pair_width : pair_width + 2].astype(F32), axis=(1, 2, 5))
    sums = jnp.transpose(sums, (1, 0, 2)).reshape(row_total)
    final = cores[..., :pair_width].reshape(2, y_count, vocab_count, y_count, own_rows, 2, block)
    final = jnp.transpose(final, (3, 0, 4, 1, 5, 2, 6)).reshape(row_total, model_width)
    final_scale = lax.rsqrt(sums / model_width + EPSILON)
    logits = lax.dot_general(final, head, (((1,), (1,)), ((), ())), preferred_element_type=F32)
    logits = logits * final_scale[:, None]

    source_of = jnp.arange(row_total, dtype=jnp.int32) % SOURCES
    parent_row = parents[0] * SOURCES + source_of
    vocab_offset = lax.axis_index(("section", "dp", "vocab")) * vocab_rows
    parent_logits = jnp.take(logits, parent_row, axis=0)
    is_pick = jnp.arange(vocab_rows, dtype=jnp.int32)[None, :] + vocab_offset == picks[0][:, None]
    picked = jnp.sum(jnp.where(is_pick, parent_logits, 0.0), axis=1)
    top = jnp.max(logits, axis=1)
    total = jnp.sum(jnp.exp(logits - top[:, None]), axis=1)
    for axes in (("dp", "vocab"), ("section",)):
        stats = jnp.stack([top, total, picked] + [jnp.zeros_like(top)] * 5)
        stats = jnp.pad(stats, ((0, 0), (0, 128 - row_total)))
        copies = jnp.broadcast_to(stats[None], (lax.axis_size(axes),) + stats.shape)
        every = lax.all_to_all(copies, axes, 0, 0, tiled=True)[:, :, :row_total]
        tops, totals, picks_of = every[:, 0], every[:, 1], every[:, 2]
        top = jnp.max(tops, axis=0)
        total = jnp.sum(totals * jnp.exp(tops - top[None]), axis=0)
        picked = jnp.sum(picks_of, axis=0)
    log_norm = top + jnp.log(total)
    scores_now = jnp.take(scores, parent_row) + picked - jnp.take(log_norm, parent_row)

    conv_next = jnp.concatenate([conv_old[:, 1:], x_kept.astype(BF16)[:, None]], axis=1)
    states = jnp.concatenate([ssm_now.astype(BF16), conv_next], axis=1)
    every = lax.all_gather(states, "dp", axis=0, tiled=False)
    beams = lax.dynamic_slice_in_dim(parents[0], dp_at * own_rows, own_rows, 0)
    mine = jnp.stack(
        [
            lax.dynamic_index_in_dim(every[:, r], beams[r], 0, keepdims=False)
            for r in range(own_rows)
        ]
    )
    ssm_new = mine[:, :STATE_DIM].astype(F32)
    return (mine[:, STATE_DIM:][None], ssm_new[None], scores_now)


def solution(mesh):
    placed = (
        P(),
        P(),
        P(),
        P(),
        P("section", ("dp", "vocab")),
        P("section", ("dp", "vocab")),
        P("section", ("dp", "vocab"), None, None),
        P("section", None, "vocab"),
        P("section", "vocab"),
        P("section", "vocab", None),
        P("section", "vocab", None),
        P("section", None, "vocab"),
        P("section", "vocab"),
        P("section", None, "vocab"),
        P("section", "vocab"),
        P("section", None, ("dp", "vocab")),
        P(),
        P(("section", "dp", "vocab"), None),
        P("section", "dp", None, "vocab"),
        P("section", "dp", None, "vocab"),
    )
    return jax.shard_map(
        on_device,
        mesh=mesh,
        in_specs=placed,
        out_specs=(P("section", "dp", None, "vocab"), P("section", "dp", None, "vocab"), P()),
        check_vma=False,
    )
```

```python
import jax
import jax.numpy as jnp
from jax import lax
from jax.experimental import pallas as pl
from jax.experimental.pallas import tpu as pltpu
from jax.sharding import PartitionSpec as P

STATE_DIM = 16
SOURCES = 4
EPSILON = 1e-05
TAIL = 128
PAD = 8

F32 = jnp.float32
BF16 = jnp.bfloat16


def by_vocab(value, by):
    n = lax.axis_size("vocab")
    return lax.ppermute(value, "vocab", [(i, (i + by) % n) for i in range(n)])


def by_y(value, by):
    n = lax.axis_size("dp") // 2
    pairs = [(2 * y + c, 2 * ((y + by) % n) + c) for y in range(n) for c in range(2)]
    return lax.ppermute(value, "dp", pairs)


def over_side(value):
    n = lax.axis_size("dp") // 2
    m = lax.axis_size("vocab")
    groups = [[(2 * y + c) * m + v for y in range(n) for v in range(m)] for c in range(2)]
    return lax.all_to_all(value, ("dp", "vocab"), 0, 0, tiled=True, axis_index_groups=groups)


def other_core(value):
    n = lax.axis_size("dp")
    return lax.ppermute(value, "dp", [(i, i ^ 1) for i in range(n)])


def next_section(value):
    n = lax.axis_size("section")
    return lax.ppermute(value, "section", [(i, (i + 1) % n) for i in range(n)])


def whole(space=pltpu.VMEM):
    return pl.BlockSpec(memory_space=space)


def place_rows(groups, at_ref, own_ref, oth_ref, hidden_ref, gain_ref):
    rows, block = own_ref.shape[1:]
    for half, ref in enumerate((own_ref, oth_ref)):
        columns = slice(half * block, (half + 1) * block)
        gain_ref[:, columns] = ref[groups, 0:1, :]
        for y in range(groups // 2):
            hidden_ref[y * rows : (y + 1) * rows, columns] = ref[2 * y + at_ref[1]]


def choose_rows(at_ref, parent_ref, own_ref, oth_ref, o0, o1, o2, o3):
    rows = own_ref.shape[0]
    y, c = at_ref[0], at_ref[1]
    for k, out in enumerate((o0, o1, o2, o3)):
        beam = 2 * lax.rem(y + 4 - k, 4) + c
        for r in range(rows):
            own = lax.rem(parent_ref[beam * rows + r], 2) == c
            picked = jnp.where(own, own_ref[r].astype(F32), oth_ref[r].astype(F32))
            out[r] = picked.astype(BF16)


def settle_rows(at_ref, parent_ref, s0, s1, s2, s3, ssm_ref, conv_ref):
    rows = s0.shape[0]
    y, c = at_ref[0], at_ref[1]
    for r in range(rows):
        parent = parent_ref[(2 * y + c) * rows + r]
        slot = lax.rem(lax.div(parent, 2) + 4 - y, 4)
        row = s0[r].astype(F32)
        for k, ref in ((1, s1), (2, s2), (3, s3)):
            row = jnp.where(slot == k, ref[r].astype(F32), row)
        ssm_ref[r] = row[:STATE_DIM]
        conv_ref[r] = row[STATE_DIM:].astype(BF16)


def project_in(columns, h_ref, gain_ref, w_ref, out_ref, scr):
    wide = w_ref.shape[1]
    rows = out_ref.shape[1]
    chan = (out_ref.shape[2] - TAIL) // 2
    sides = wide // (2 * chan)
    hidden = h_ref[...]
    normed = (hidden * gain_ref[...]).astype(BF16)
    squares = jnp.sum(hidden * hidden, axis=1, keepdims=True)
    high = squares.astype(BF16).astype(F32)
    lane = lax.broadcasted_iota(jnp.int32, (hidden.shape[0], TAIL), 1)
    scr[:, wide:] = jnp.where(lane == 0, high, jnp.where(lane == 1, squares - high, 0.0))
    for at in range(0, wide, columns):
        there = slice(at, at + columns)
        scr[:, there] = jnp.dot(normed, w_ref[:, there], preferred_element_type=F32)
    for y in range(out_ref.shape[0] // sides):
        own = slice(y * rows, (y + 1) * rows)
        for v in range(sides):
            for half in range(2):
                at = (half * sides + v) * chan
                out_ref[y * sides + v, :, half * chan : (half + 1) * chan] = scr[
                    own, at : at + chan
                ].astype(BF16)
            out_ref[y * sides + v, :, 2 * chan :] = scr[own, wide:].astype(BF16)


def convolve(model_width, sums_ref, small_ref, w_x, part_ref, side_ref):
    total = sums_ref[0].astype(F32)
    for i in range(1, sums_ref.shape[0]):
        total = total + sums_ref[i].astype(F32)
    rows = total.shape[0]
    wide = total.shape[1] - TAIL
    half = wide // 2
    squares = total[:, wide : wide + 1] + total[:, wide + 1 : wide + 2]
    scale = lax.rsqrt(squares / model_width + EPSILON)
    projected = (total[:, :wide] * scale).astype(BF16).astype(F32)
    x = projected[:, :half]
    z = projected[:, half:]
    act = jax.nn.silu(small_ref[0:rows, :] + x * small_ref[rows : rows + 1, :])
    part_ref[...] = jnp.dot(act.astype(BF16), w_x[...], preferred_element_type=F32)
    side_ref[0] = act
    side_ref[1] = jax.nn.silu(z)
    side_ref[2] = x


def advance(
    section, at_ref, p0, p1, p2, p3, side_ref, w_dt, small_ref, x_in, ssm_in,
    mixed_ref, x_out, ssm_out, scr,
):
    terms = p0[...] + p1[...] + p2[...] + p3[...]
    rank = w_dt.shape[0]
    rows = terms.shape[0]
    low = terms[:, :rank].astype(BF16)
    pre = jnp.dot(low, w_dt[...], preferred_element_type=F32)
    pre = pre + small_ref[rows + 1 : rows + 2, :]
    step = jnp.maximum(pre, 0.0) + jnp.log1p(jnp.exp(-jnp.abs(pre)))
    act = side_ref[0]
    scr[0] = step
    scr[1] = step * act
    bc = terms[:, rank : rank + 2 * STATE_DIM]
    shape = (STATE_DIM, 2 * STATE_DIM)
    lane = lax.broadcasted_iota(jnp.int32, shape, 1)
    sub = lax.broadcasted_iota(jnp.int32, shape, 0)
    rates = small_ref[PAD:, :]
    live = at_ref[3] == section
    for g in range(rows):
        line = jnp.broadcast_to(bc[g : g + 1, :], shape)
        b_col = jnp.sum(jnp.where(lane == sub, line, 0.0), axis=1, keepdims=True)
        c_col = jnp.sum(jnp.where(lane == sub + STATE_DIM, line, 0.0), axis=1, keepdims=True)
        old = ssm_in[g]
        new = jnp.exp(-scr[0, g : g + 1, :] * rates) * old + b_col * scr[1, g : g + 1, :]
        scr[2, g : g + 1, :] = jnp.sum(c_col * new, axis=0, keepdims=True)
        ssm_out[g] = jnp.where(live, new, old)
    x_out[...] = jnp.where(live, side_ref[2], x_in[...])
    mixed = (scr[2] + small_ref[rows + 2 : rows + 3, :] * act) * side_ref[1]
    mixed = mixed.astype(BF16)
    for i in range(mixed_ref.shape[0]):
        mixed_ref[i] = mixed


def project_out(sides, m_ref, h_ref, w_ref, out_ref, scr):
    rows, chan = m_ref.shape[1:]
    total = h_ref[...]
    for v in range(sides):
        for y in range(m_ref.shape[0] // sides):
            scr[y * rows : (y + 1) * rows, :] = m_ref[y * sides + v].astype(F32)
        total = total + jnp.dot(
            scr[...].astype(BF16),
            w_ref[v * chan : (v + 1) * chan, :],
            preferred_element_type=F32,
        )
    out_ref[...] = total


def finish(at_ref, h_ref, gain_ref, out_ref):
    rows = h_ref[...]
    width = rows.shape[1]
    half = width // 2
    first = at_ref[1] == 0
    left = jnp.where(first, rows[:, :half], rows[:, half:])
    right = jnp.where(first, rows[:, half:], rows[:, :half])
    out_ref[:, :half] = (left * gain_ref[:, :half]).astype(BF16)
    out_ref[:, half:width] = (right * gain_ref[:, half:]).astype(BF16)
    squares = jnp.sum(rows * rows, axis=1, keepdims=True)
    high = squares.astype(BF16).astype(F32)
    lane = lax.broadcasted_iota(jnp.int32, (rows.shape[0], TAIL), 1)
    tail = jnp.where(lane == 0, high, jnp.where(lane == 1, squares - high, 0.0))
    out_ref[:, width:] = tail.astype(BF16)


def local_call(body, outs, scratch=(), smem=0, operands=0, aliases=None, cost=None):
    specs = [whole(pltpu.SMEM)] * smem + [whole()] * (operands - smem)
    return pl.pallas_call(
        body,
        out_shape=[jax.ShapeDtypeStruct(shape, dtype) for shape, dtype in outs],
        in_specs=specs,
        out_specs=[whole()] * len(outs),
        scratch_shapes=[pltpu.VMEM(shape, F32) for shape in scratch],
        input_output_aliases=aliases or {},
        compiler_params=pltpu.CompilerParams(vmem_limit_bytes=12 * 2**20),
        cost_estimate=cost,
    )


def on_device(
    tokens_in,
    picks,
    parents,
    scores,
    embed,
    norm_gain,
    in_weight,
    conv_weight,
    conv_bias,
    xdt_weight,
    xbc_weight,
    dt_weight,
    dt_bias,
    a_rate,
    skip,
    out_weight,
    final_gain,
    head,
    conv_state,
    ssm_state,
):
    section_count = lax.axis_size("section")
    dp_count = lax.axis_size("dp")
    vocab_count = lax.axis_size("vocab")
    y_count = dp_count // 2
    row_total = tokens_in.shape[0]
    own_rows = row_total // dp_count
    core_rows = own_rows * y_count
    section_at = lax.axis_index("section")
    dp_at = lax.axis_index("dp")
    vocab_at = lax.axis_index("vocab")
    y_at = dp_at // 2
    core_at = dp_at % 2
    block = in_weight.shape[1]
    chan = in_weight.shape[3] // vocab_count
    model_width = final_gain.shape[0]
    pair_width = 2 * block
    sides = y_count * vocab_count
    vocab_rows = head.shape[0]

    coords = jnp.stack([y_at, core_at, vocab_at, section_at]).astype(jnp.int32)

    embed_rows = embed.shape[0]
    local_ids = tokens_in - section_at * embed_rows
    inside = (local_ids >= 0) & (local_ids < embed_rows)
    found = jnp.take(embed, jnp.clip(local_ids, 0, embed_rows - 1), axis=0)
    found = jnp.where(inside[:, None], found, 0).astype(BF16)
    found, in_own, ssm_now = lax.optimization_barrier((found, in_weight[0], ssm_state[0]))
    copies = jnp.broadcast_to(found[None], (section_count,) + found.shape)
    pieces = lax.all_to_all(copies, "section", 0, 0, tiled=True)
    looked_up = jnp.sum(pieces.astype(F32), axis=0).reshape(dp_count, own_rows, block)
    beside = jnp.pad(norm_gain, ((0, own_rows - 1), (0, 0)))
    bundle = jnp.concatenate([looked_up, beside[None]], axis=0)
    hidden, gain = local_call(
        lambda *refs: place_rows(dp_count, *refs),
        [((core_rows, pair_width), F32), ((1, pair_width), F32)],
        smem=1,
        operands=3,
    )(coords, bundle, other_core(bundle))

    in_own = in_own.reshape(block, 2 * vocab_count * chan)
    w_in = jnp.concatenate([in_own, other_core(in_own)], axis=0)
    w_out = jnp.concatenate([out_weight[0], other_core(out_weight[0])], axis=1)

    w_x = jnp.concatenate([xdt_weight[0], xbc_weight[0]], axis=1)
    w_dt = dt_weight[0]
    taps = conv_weight[0]
    conv_old = conv_state[0]
    keep = taps.shape[0] - 1
    conv_pre = conv_bias + jnp.sum(conv_old.astype(F32) * taps[None, :keep], axis=1)
    small = jnp.concatenate(
        [conv_pre, taps[keep:], dt_bias, skip, jnp.zeros((1, chan), F32), a_rate[0]], axis=0
    )
    x_kept = jnp.zeros((own_rows, chan), F32)

    wide = 2 * chan + TAIL
    terms_wide = w_x.shape[1]
    call_in = local_call(
        lambda *refs: project_in(512, *refs),
        [((sides, own_rows, wide), BF16)],
        scratch=[(core_rows, 2 * vocab_count * chan + TAIL)],
        operands=3,
        cost=pl.CostEstimate(
            flops=4 * core_rows * pair_width * vocab_count * chan,
            bytes_accessed=4 * pair_width * vocab_count * chan,
            transcendentals=0,
        ),
    )
    call_conv = local_call(
        lambda *refs: convolve(model_width, *refs),
        [((own_rows, terms_wide), F32), ((3, own_rows, chan), F32)],
        operands=3,
        cost=pl.CostEstimate(
            flops=2 * own_rows * chan * terms_wide,
            bytes_accessed=2 * chan * terms_wide,
            transcendentals=2 * own_rows * chan,
        ),
    )
    def call_state(section, *operands):
        return local_call(
            lambda *refs: advance(section, *refs),
            [((sides, own_rows, chan), BF16), ((own_rows, chan), F32), (ssm_now.shape, F32)],
            scratch=[(3, own_rows, chan)],
            smem=1,
            operands=10,
            aliases={8: 1, 9: 2},
            cost=pl.CostEstimate(
                flops=2 * own_rows * chan * dt_weight.shape[1],
                bytes_accessed=2 * chan * dt_weight.shape[1] + 8 * ssm_now.size,
                transcendentals=ssm_now.size,
            ),
        )(*operands)

    call_out = local_call(
        lambda *refs: project_out(vocab_count, *refs),
        [((core_rows, pair_width), F32)],
        scratch=[(core_rows, chan)],
        operands=3,
        cost=pl.CostEstimate(
            flops=2 * core_rows * pair_width * vocab_count * chan,
            bytes_accessed=2 * pair_width * vocab_count * chan,
            transcendentals=0,
        ),
    )

    for step in range(section_count):
        (parts,) = call_in(hidden, gain, w_in)
        terms, side = call_conv(over_side(parts), small, w_x)
        all_terms = [terms] + [by_vocab(terms, k) for k in range(1, vocab_count)]
        mixed, x_kept, ssm_now = call_state(
            step, coords, *all_terms, side, w_dt, small, x_kept, ssm_now
        )
        (hidden,) = call_out(over_side(mixed), hidden, w_out)
        if step + 1 < section_count:
            hidden = next_section(hidden)

    pair_gain = final_gain.reshape(y_count, 2, vocab_count, block)
    pair_gain = lax.dynamic_index_in_dim(pair_gain, y_at, 0, keepdims=False)
    pair_gain = lax.dynamic_index_in_dim(pair_gain, vocab_at, 1, keepdims=False)
    (sent,) = local_call(
        finish,
        [((core_rows, pair_width + TAIL), BF16)],
        smem=1,
        operands=3,
    )(coords, hidden, pair_gain.reshape(1, pair_width))
    last = section_count - 1
    middle = last // 2
    got = lax.ppermute(sent, "section", [(last, middle)])
    sent = jnp.where(section_at == middle, got, sent)
    received = jnp.zeros_like(sent)
    for k in range(1, middle + 1):
        pairs = [(last, (last + k) % section_count), (middle, middle + k)]
        received = received + lax.ppermute(sent, "section", pairs)
    _, ssm_now, x_kept = lax.optimization_barrier((got, ssm_now, x_kept))
    conv_next = jnp.concatenate([conv_old[:, 1:], x_kept.astype(BF16)[:, None]], axis=1)
    states = jnp.concatenate([ssm_now.astype(BF16), conv_next], axis=1)
    chosen = local_call(
        choose_rows,
        [(states.shape, BF16)] * y_count,
        smem=2,
        operands=4,
    )(coords, parents[0], states, other_core(states))
    chosen = [chosen[0]] + [by_y(chosen[k], -k) for k in range(1, y_count)]
    ssm_new, conv_new = local_call(
        settle_rows,
        [(ssm_now.shape, F32), (conv_next.shape, BF16)],
        smem=2,
        operands=6,
    )(coords, parents[0], *chosen)
    is_source = (section_at == middle) | (section_at == last)
    sent = jnp.where(is_source, sent, received)
    every = over_side(jnp.broadcast_to(sent[None], (sides,) + sent.shape))
    facing = other_core(every)
    cores = jnp.where(core_at == 0, jnp.stack([every, facing]), jnp.stack([facing, every]))
    cores = cores.reshape(2, y_count, vocab_count, y_count, own_rows, pair_width + TAIL)
    sums = jnp.sum(cores[..., pair_width : pair_width + 2].astype(F32), axis=(1, 2, 5))
    sums = jnp.transpose(sums, (1, 0, 2)).reshape(row_total)
    final = cores[..., :pair_width].reshape(2, y_count, vocab_count, y_count, own_rows, 2, block)
    final = jnp.transpose(final, (3, 0, 4, 1, 5, 2, 6)).reshape(row_total, model_width)
    final_scale = lax.rsqrt(sums / model_width + EPSILON)
    logits = lax.dot_general(final, head, (((1,), (1,)), ((), ())), preferred_element_type=F32)
    logits = logits * final_scale[:, None]

    source_of = jnp.arange(row_total, dtype=jnp.int32) % SOURCES
    parent_row = parents[0] * SOURCES + source_of
    vocab_offset = lax.axis_index(("section", "dp", "vocab")) * vocab_rows
    parent_logits = jnp.take(logits, parent_row, axis=0)
    is_pick = jnp.arange(vocab_rows, dtype=jnp.int32)[None, :] + vocab_offset == picks[0][:, None]
    picked = jnp.sum(jnp.where(is_pick, parent_logits, 0.0), axis=1)
    top = jnp.max(logits, axis=1)
    total = jnp.sum(jnp.exp(logits - top[:, None]), axis=1)
    for axes in (("dp", "vocab"), ("section",)):
        stats = jnp.stack([top, total, picked] + [jnp.zeros_like(top)] * 5)
        stats = jnp.pad(stats, ((0, 0), (0, 128 - row_total)))
        copies = jnp.broadcast_to(stats[None], (lax.axis_size(axes),) + stats.shape)
        every = lax.all_to_all(copies, axes, 0, 0, tiled=True)[:, :, :row_total]
        tops, totals, picks_of = every[:, 0], every[:, 1], every[:, 2]
        top = jnp.max(tops, axis=0)
        total = jnp.sum(totals * jnp.exp(tops - top[None]), axis=0)
        picked = jnp.sum(picks_of, axis=0)
    log_norm = top + jnp.log(total)
    scores_now = jnp.take(scores, parent_row) + picked - jnp.take(log_norm, parent_row)

    return (conv_new[None], ssm_new[None], scores_now)


def solution(mesh):
    placed = (
        P(),
        P(),
        P(),
        P(),
        P("section", ("dp", "vocab")),
        P("section", ("dp", "vocab")),
        P("section", ("dp", "vocab"), None, None),
        P("section", None, "vocab"),
        P("section", "vocab"),
        P("section", "vocab", None),
        P("section", "vocab", None),
        P("section", None, "vocab"),
        P("section", "vocab"),
        P("section", None, "vocab"),
        P("section", "vocab"),
        P("section", None, ("dp", "vocab")),
        P(),
        P(("section", "dp", "vocab"), None),
        P("section", "dp", None, "vocab"),
        P("section", "dp", None, "vocab"),
    )
    return jax.shard_map(
        on_device,
        mesh=mesh,
        in_specs=placed,
        out_specs=(P("section", "dp", None, "vocab"), P("section", "dp", None, "vocab"), P()),
        check_vma=False,
    )
```

```python
import jax
import jax.numpy as jnp
from jax import lax
from jax.experimental import pallas as pl
from jax.experimental.pallas import tpu as pltpu
from jax.sharding import PartitionSpec as P

STATE_DIM = 16
SOURCES = 4
EPSILON = 1e-05
TAIL = 128
PAD = 8

F32 = jnp.float32
BF16 = jnp.bfloat16


def by_vocab(value, by):
    n = lax.axis_size("vocab")
    return lax.ppermute(value, "vocab", [(i, (i + by) % n) for i in range(n)])


def by_y(value, by):
    n = lax.axis_size("dp") // 2
    pairs = [(2 * y + c, 2 * ((y + by) % n) + c) for y in range(n) for c in range(2)]
    return lax.ppermute(value, "dp", pairs)


def over_side(value):
    n = lax.axis_size("dp") // 2
    m = lax.axis_size("vocab")
    groups = [[(2 * y + c) * m + v for y in range(n) for v in range(m)] for c in range(2)]
    return lax.all_to_all(value, ("dp", "vocab"), 0, 0, tiled=True, axis_index_groups=groups)


def other_core(value):
    n = lax.axis_size("dp")
    return lax.ppermute(value, "dp", [(i, i ^ 1) for i in range(n)])


def next_section(value):
    n = lax.axis_size("section")
    return lax.ppermute(value, "section", [(i, (i + 1) % n) for i in range(n)])


def whole(space=pltpu.VMEM):
    return pl.BlockSpec(memory_space=space)


def place_rows(groups, at_ref, own_ref, oth_ref, hidden_ref, gain_ref):
    rows, block = own_ref.shape[1:]
    for half, ref in enumerate((own_ref, oth_ref)):
        columns = slice(half * block, (half + 1) * block)
        gain_ref[:, columns] = ref[groups, 0:1, :]
        for y in range(groups // 2):
            hidden_ref[y * rows : (y + 1) * rows, columns] = ref[2 * y + at_ref[1]]


def choose_rows(at_ref, parent_ref, own_ref, oth_ref, o0, o1, o2, o3):
    rows = own_ref.shape[0]
    y, c = at_ref[0], at_ref[1]
    for k, out in enumerate((o0, o1, o2, o3)):
        beam = 2 * lax.rem(y + 4 - k, 4) + c
        for r in range(rows):
            own = lax.rem(parent_ref[beam * rows + r], 2) == c
            picked = jnp.where(own, own_ref[r].astype(F32), oth_ref[r].astype(F32))
            out[r] = picked.astype(BF16)


def settle_rows(at_ref, parent_ref, s0, s1, s2, s3, ssm_ref, conv_ref):
    rows = s0.shape[0]
    y, c = at_ref[0], at_ref[1]
    for r in range(rows):
        parent = parent_ref[(2 * y + c) * rows + r]
        slot = lax.rem(lax.div(parent, 2) + 4 - y, 4)
        row = s0[r].astype(F32)
        for k, ref in ((1, s1), (2, s2), (3, s3)):
            row = jnp.where(slot == k, ref[r].astype(F32), row)
        ssm_ref[r] = row[:STATE_DIM]
        conv_ref[r] = row[STATE_DIM:].astype(BF16)


def project_in(columns, h_ref, gain_ref, w_ref, out_ref, scr):
    wide = w_ref.shape[1]
    rows = out_ref.shape[1]
    sides = 4
    chan = (out_ref.shape[2] - TAIL) // (sides + 1)
    hidden = h_ref[...]
    normed = (hidden * gain_ref[...]).astype(BF16)
    squares = jnp.sum(hidden * hidden, axis=1, keepdims=True)
    high = squares.astype(BF16).astype(F32)
    lane = lax.broadcasted_iota(jnp.int32, (hidden.shape[0], TAIL), 1)
    scr[:, wide:] = jnp.where(lane == 0, high, jnp.where(lane == 1, squares - high, 0.0))
    for at in range(0, wide, columns):
        there = slice(at, at + columns)
        scr[:, there] = jnp.dot(normed, w_ref[:, there], preferred_element_type=F32)
    for y in range(out_ref.shape[0] // sides):
        own = slice(y * rows, (y + 1) * rows)
        for v in range(sides):
            place = y * sides + v
            for j in range(sides):
                at = ((v - j) % sides) * chan
                out_ref[place, :, j * chan : (j + 1) * chan] = scr[own, at : at + chan].astype(BF16)
            at = (sides + v) * chan
            there = slice(sides * chan, (sides + 1) * chan)
            out_ref[place, :, there] = scr[own, at : at + chan].astype(BF16)
            out_ref[place, :, (sides + 1) * chan :] = scr[own, wide:].astype(BF16)


def advance(
    section, model_width, at_ref, sums_ref, small_ref, c1, c2, c3, x0, x1, x2, x3, w_dt, x_in, ssm_in,
    mixed_ref, x_out, ssm_out, scr,
):
    total = sums_ref[0].astype(F32)
    for i in range(1, sums_ref.shape[0]):
        total = total + sums_ref[i].astype(F32)
    rows = total.shape[0]
    chan = w_dt.shape[1]
    wide = total.shape[1] - TAIL
    squares = total[:, wide : wide + 1] + total[:, wide + 1 : wide + 2]
    scale = lax.rsqrt(squares / model_width + EPSILON)
    projected = (total[:, :wide] * scale).astype(BF16).astype(F32)
    acts = []
    terms = jnp.zeros((rows, x0.shape[1]), F32)
    for j, (conv, w) in enumerate(zip((small_ref, c1, c2, c3), (x0, x1, x2, x3))):
        x = projected[:, j * chan : (j + 1) * chan]
        acts.append(jax.nn.silu(conv[0:rows, :] + x * conv[rows : rows + 1, :]))
        terms = terms + jnp.dot(acts[j].astype(BF16), w[...], preferred_element_type=F32)
    act = acts[0]
    gate = jax.nn.silu(projected[:, wide - chan :])
    rank = w_dt.shape[0]
    low = terms[:, :rank].astype(BF16)
    pre = jnp.dot(low, w_dt[...], preferred_element_type=F32)
    pre = pre + small_ref[rows + 1 : rows + 2, :]
    step = jnp.maximum(pre, 0.0) + jnp.log1p(jnp.exp(-jnp.abs(pre)))
    scr[0] = step
    scr[1] = step * act
    bc = terms[:, rank : rank + 2 * STATE_DIM]
    shape = (STATE_DIM, 2 * STATE_DIM)
    lane = lax.broadcasted_iota(jnp.int32, shape, 1)
    sub = lax.broadcasted_iota(jnp.int32, shape, 0)
    rates = small_ref[PAD:, :]
    live = at_ref[3] == section
    for g in range(rows):
        line = jnp.broadcast_to(bc[g : g + 1, :], shape)
        b_col = jnp.sum(jnp.where(lane == sub, line, 0.0), axis=1, keepdims=True)
        c_col = jnp.sum(jnp.where(lane == sub + STATE_DIM, line, 0.0), axis=1, keepdims=True)
        old = ssm_in[g]
        new = jnp.exp(-scr[0, g : g + 1, :] * rates) * old + b_col * scr[1, g : g + 1, :]
        scr[2, g : g + 1, :] = jnp.sum(c_col * new, axis=0, keepdims=True)
        ssm_out[g] = jnp.where(live, new, old)
    x_out[...] = jnp.where(live, projected[:, :chan], x_in[...])
    mixed = (scr[2] + small_ref[rows + 2 : rows + 3, :] * act) * gate
    mixed = mixed.astype(BF16)
    for i in range(mixed_ref.shape[0]):
        mixed_ref[i] = mixed


def project_out(sides, m_ref, h_ref, w_ref, out_ref, scr):
    rows, chan = m_ref.shape[1:]
    total = h_ref[...]
    for v in range(sides):
        for y in range(m_ref.shape[0] // sides):
            scr[y * rows : (y + 1) * rows, :] = m_ref[y * sides + v].astype(F32)
        total = total + jnp.dot(
            scr[...].astype(BF16),
            w_ref[v * chan : (v + 1) * chan, :],
            preferred_element_type=F32,
        )
    out_ref[...] = total


def finish(at_ref, h_ref, gain_ref, out_ref):
    rows = h_ref[...]
    width = rows.shape[1]
    half = width // 2
    first = at_ref[1] == 0
    left = jnp.where(first, rows[:, :half], rows[:, half:])
    right = jnp.where(first, rows[:, half:], rows[:, :half])
    out_ref[:, :half] = (left * gain_ref[:, :half]).astype(BF16)
    out_ref[:, half:width] = (right * gain_ref[:, half:]).astype(BF16)
    squares = jnp.sum(rows * rows, axis=1, keepdims=True)
    high = squares.astype(BF16).astype(F32)
    lane = lax.broadcasted_iota(jnp.int32, (rows.shape[0], TAIL), 1)
    tail = jnp.where(lane == 0, high, jnp.where(lane == 1, squares - high, 0.0))
    out_ref[:, width:] = tail.astype(BF16)


def local_call(body, outs, scratch=(), smem=0, operands=0, aliases=None, cost=None):
    specs = [whole(pltpu.SMEM)] * smem + [whole()] * (operands - smem)
    return pl.pallas_call(
        body,
        out_shape=[jax.ShapeDtypeStruct(shape, dtype) for shape, dtype in outs],
        in_specs=specs,
        out_specs=[whole()] * len(outs),
        scratch_shapes=[pltpu.VMEM(shape, F32) for shape in scratch],
        input_output_aliases=aliases or {},
        compiler_params=pltpu.CompilerParams(vmem_limit_bytes=12 * 2**20),
        cost_estimate=cost,
    )


def on_device(
    tokens_in,
    picks,
    parents,
    scores,
    embed,
    norm_gain,
    in_weight,
    conv_weight,
    conv_bias,
    xdt_weight,
    xbc_weight,
    dt_weight,
    dt_bias,
    a_rate,
    skip,
    out_weight,
    final_gain,
    head,
    conv_state,
    ssm_state,
):
    section_count = lax.axis_size("section")
    dp_count = lax.axis_size("dp")
    vocab_count = lax.axis_size("vocab")
    y_count = dp_count // 2
    row_total = tokens_in.shape[0]
    own_rows = row_total // dp_count
    core_rows = own_rows * y_count
    section_at = lax.axis_index("section")
    dp_at = lax.axis_index("dp")
    vocab_at = lax.axis_index("vocab")
    y_at = dp_at // 2
    core_at = dp_at % 2
    block = in_weight.shape[1]
    chan = in_weight.shape[3] // vocab_count
    model_width = final_gain.shape[0]
    pair_width = 2 * block
    sides = y_count * vocab_count
    vocab_rows = head.shape[0]

    coords = jnp.stack([y_at, core_at, vocab_at, section_at]).astype(jnp.int32)

    embed_rows = embed.shape[0]
    local_ids = tokens_in - section_at * embed_rows
    inside = (local_ids >= 0) & (local_ids < embed_rows)
    found = jnp.take(embed, jnp.clip(local_ids, 0, embed_rows - 1), axis=0)
    found = jnp.where(inside[:, None], found, 0).astype(BF16)
    found, in_own, ssm_now = lax.optimization_barrier((found, in_weight[0], ssm_state[0]))
    copies = jnp.broadcast_to(found[None], (section_count,) + found.shape)
    pieces = lax.all_to_all(copies, "section", 0, 0, tiled=True)
    looked_up = jnp.sum(pieces.astype(F32), axis=0).reshape(dp_count, own_rows, block)
    beside = jnp.pad(norm_gain, ((0, own_rows - 1), (0, 0)))
    bundle = jnp.concatenate([looked_up, beside[None]], axis=0)
    hidden, gain = local_call(
        lambda *refs: place_rows(dp_count, *refs),
        [((core_rows, pair_width), F32), ((1, pair_width), F32)],
        smem=1,
        operands=3,
    )(coords, bundle, other_core(bundle))

    in_own = in_own.reshape(block, 2 * vocab_count * chan)
    w_in = jnp.concatenate([in_own, other_core(in_own)], axis=0)
    w_out = jnp.concatenate([out_weight[0], other_core(out_weight[0])], axis=1)

    w_x = jnp.concatenate([xdt_weight[0], xbc_weight[0]], axis=1)
    w_dt = dt_weight[0]
    taps = conv_weight[0]
    conv_old = conv_state[0]
    keep = taps.shape[0] - 1
    conv_pre = conv_bias + jnp.sum(conv_old.astype(F32) * taps[None, :keep], axis=1)
    small = jnp.concatenate(
        [conv_pre, taps[keep:], dt_bias, skip, jnp.zeros((1, chan), F32), a_rate[0]], axis=0
    )
    x_kept = jnp.zeros((own_rows, chan), F32)

    wide = (vocab_count + 1) * chan + TAIL
    _, w_x = lax.optimization_barrier((found, w_x))
    all_x = [w_x] + [by_vocab(w_x, k) for k in range(1, vocab_count)]
    all_conv = [by_vocab(small[:PAD], k) for k in range(1, vocab_count)]
    call_in = local_call(
        lambda *refs: project_in(512, *refs),
        [((sides, own_rows, wide), BF16)],
        scratch=[(core_rows, 2 * vocab_count * chan + TAIL)],
        operands=3,
        cost=pl.CostEstimate(
            flops=4 * core_rows * pair_width * vocab_count * chan,
            bytes_accessed=4 * pair_width * vocab_count * chan,
            transcendentals=0,
        ),
    )
    def call_state(section, *operands):
        return local_call(
            lambda *refs: advance(section, model_width, *refs),
            [((sides, own_rows, chan), BF16), ((own_rows, chan), F32), (ssm_now.shape, F32)],
            scratch=[(3, own_rows, chan)],
            smem=1,
            operands=13,
            aliases={11: 1, 12: 2},
            cost=pl.CostEstimate(
                flops=10 * own_rows * chan * dt_weight.shape[1],
                bytes_accessed=10 * chan * dt_weight.shape[1] + 8 * ssm_now.size,
                transcendentals=ssm_now.size,
            ),
        )(*operands)

    call_out = local_call(
        lambda *refs: project_out(vocab_count, *refs),
        [((core_rows, pair_width), F32)],
        scratch=[(core_rows, chan)],
        operands=3,
        cost=pl.CostEstimate(
            flops=2 * core_rows * pair_width * vocab_count * chan,
            bytes_accessed=2 * pair_width * vocab_count * chan,
            transcendentals=0,
        ),
    )

    for step in range(section_count):
        (parts,) = call_in(hidden, gain, w_in)
        if step == 0:
            _, all_x, w_out = lax.optimization_barrier((parts, all_x, w_out))
        mixed, x_kept, ssm_now = call_state(
            step, coords, over_side(parts), small, *all_conv, *all_x, w_dt, x_kept, ssm_now
        )
        (hidden,) = call_out(over_side(mixed), hidden, w_out)
        if step + 1 < section_count:
            hidden = next_section(hidden)

    pair_gain = final_gain.reshape(y_count, 2, vocab_count, block)
    pair_gain = lax.dynamic_index_in_dim(pair_gain, y_at, 0, keepdims=False)
    pair_gain = lax.dynamic_index_in_dim(pair_gain, vocab_at, 1, keepdims=False)
    (sent,) = local_call(
        finish,
        [((core_rows, pair_width + TAIL), BF16)],
        smem=1,
        operands=3,
    )(coords, hidden, pair_gain.reshape(1, pair_width))
    last = section_count - 1
    middle = last // 2
    got = lax.ppermute(sent, "section", [(last, middle)])
    sent = jnp.where(section_at == middle, got, sent)
    received = jnp.zeros_like(sent)
    for k in range(1, middle + 1):
        pairs = [(last, (last + k) % section_count), (middle, middle + k)]
        received = received + lax.ppermute(sent, "section", pairs)
    _, ssm_now, x_kept = lax.optimization_barrier((got, ssm_now, x_kept))
    conv_next = jnp.concatenate([conv_old[:, 1:], x_kept.astype(BF16)[:, None]], axis=1)
    states = jnp.concatenate([ssm_now.astype(BF16), conv_next], axis=1)
    chosen = local_call(
        choose_rows,
        [(states.shape, BF16)] * y_count,
        smem=2,
        operands=4,
    )(coords, parents[0], states, other_core(states))
    chosen = [chosen[0]] + [by_y(chosen[k], -k) for k in range(1, y_count)]
    ssm_new, conv_new = local_call(
        settle_rows,
        [(ssm_now.shape, F32), (conv_next.shape, BF16)],
        smem=2,
        operands=6,
    )(coords, parents[0], *chosen)
    is_source = (section_at == middle) | (section_at == last)
    sent = jnp.where(is_source, sent, received)
    every = over_side(jnp.broadcast_to(sent[None], (sides,) + sent.shape))
    facing = other_core(every)
    cores = jnp.where(core_at == 0, jnp.stack([every, facing]), jnp.stack([facing, every]))
    cores = cores.reshape(2, y_count, vocab_count, y_count, own_rows, pair_width + TAIL)
    sums = jnp.sum(cores[..., pair_width : pair_width + 2].astype(F32), axis=(1, 2, 5))
    sums = jnp.transpose(sums, (1, 0, 2)).reshape(row_total)
    final = cores[..., :pair_width].reshape(2, y_count, vocab_count, y_count, own_rows, 2, block)
    final = jnp.transpose(final, (3, 0, 4, 1, 5, 2, 6)).reshape(row_total, model_width)
    final_scale = lax.rsqrt(sums / model_width + EPSILON)
    logits = lax.dot_general(final, head, (((1,), (1,)), ((), ())), preferred_element_type=F32)
    logits = logits * final_scale[:, None]

    source_of = jnp.arange(row_total, dtype=jnp.int32) % SOURCES
    parent_row = parents[0] * SOURCES + source_of
    vocab_offset = lax.axis_index(("section", "dp", "vocab")) * vocab_rows
    parent_logits = jnp.take(logits, parent_row, axis=0)
    is_pick = jnp.arange(vocab_rows, dtype=jnp.int32)[None, :] + vocab_offset == picks[0][:, None]
    picked = jnp.sum(jnp.where(is_pick, parent_logits, 0.0), axis=1)
    top = jnp.max(logits, axis=1)
    total = jnp.sum(jnp.exp(logits - top[:, None]), axis=1)
    for axes in (("dp", "vocab"), ("section",)):
        stats = jnp.stack([top, total, picked] + [jnp.zeros_like(top)] * 5)
        stats = jnp.pad(stats, ((0, 0), (0, 128 - row_total)))
        copies = jnp.broadcast_to(stats[None], (lax.axis_size(axes),) + stats.shape)
        every = lax.all_to_all(copies, axes, 0, 0, tiled=True)[:, :, :row_total]
        tops, totals, picks_of = every[:, 0], every[:, 1], every[:, 2]
        top = jnp.max(tops, axis=0)
        total = jnp.sum(totals * jnp.exp(tops - top[None]), axis=0)
        picked = jnp.sum(picks_of, axis=0)
    log_norm = top + jnp.log(total)
    scores_now = jnp.take(scores, parent_row) + picked - jnp.take(log_norm, parent_row)

    return (conv_new[None], ssm_new[None], scores_now)


def solution(mesh):
    placed = (
        P(),
        P(),
        P(),
        P(),
        P("section", ("dp", "vocab")),
        P("section", ("dp", "vocab")),
        P("section", ("dp", "vocab"), None, None),
        P("section", None, "vocab"),
        P("section", "vocab"),
        P("section", "vocab", None),
        P("section", "vocab", None),
        P("section", None, "vocab"),
        P("section", "vocab"),
        P("section", None, "vocab"),
        P("section", "vocab"),
        P("section", None, ("dp", "vocab")),
        P(),
        P(("section", "dp", "vocab"), None),
        P("section", "dp", None, "vocab"),
        P("section", "dp", None, "vocab"),
    )
    return jax.shard_map(
        on_device,
        mesh=mesh,
        in_specs=placed,
        out_specs=(P("section", "dp", None, "vocab"), P("section", "dp", None, "vocab"), P()),
        check_vma=False,
    )
```

```python
import jax
import jax.numpy as jnp
from jax import lax
from jax.experimental import pallas as pl
from jax.experimental.pallas import tpu as pltpu
from jax.sharding import PartitionSpec as P

STATE_DIM = 16
SOURCES = 4
EPSILON = 1e-05
TAIL = 128
PAD = 8

F32 = jnp.float32
BF16 = jnp.bfloat16


def by_vocab(value, by):
    n = lax.axis_size("vocab")
    return lax.ppermute(value, "vocab", [(i, (i + by) % n) for i in range(n)])


def by_y(value, by):
    n = lax.axis_size("dp") // 2
    pairs = [(2 * y + c, 2 * ((y + by) % n) + c) for y in range(n) for c in range(2)]
    return lax.ppermute(value, "dp", pairs)


def over_side(value):
    n = lax.axis_size("dp") // 2
    m = lax.axis_size("vocab")
    groups = [[(2 * y + c) * m + v for y in range(n) for v in range(m)] for c in range(2)]
    return lax.all_to_all(value, ("dp", "vocab"), 0, 0, tiled=True, axis_index_groups=groups)


def other_core(value):
    n = lax.axis_size("dp")
    return lax.ppermute(value, "dp", [(i, i ^ 1) for i in range(n)])


def next_section(value):
    n = lax.axis_size("section")
    return lax.ppermute(value, "section", [(i, (i + 1) % n) for i in range(n)])


def whole(space=pltpu.VMEM):
    return pl.BlockSpec(memory_space=space)


def place_rows(groups, at_ref, own_ref, oth_ref, hidden_ref, gain_ref):
    rows, block = own_ref.shape[1:]
    for half, ref in enumerate((own_ref, oth_ref)):
        columns = slice(half * block, (half + 1) * block)
        gain_ref[:, columns] = ref[groups, 0:1, :]
        for y in range(groups // 2):
            hidden_ref[y * rows : (y + 1) * rows, columns] = ref[2 * y + at_ref[1]]


def choose_rows(at_ref, parent_ref, own_ref, oth_ref, o0, o1, o2, o3):
    rows = own_ref.shape[0]
    y, c = at_ref[0], at_ref[1]
    for k, out in enumerate((o0, o1, o2, o3)):
        beam = 2 * lax.rem(y + 4 - k, 4) + c
        for r in range(rows):
            own = lax.rem(parent_ref[beam * rows + r], 2) == c
            picked = jnp.where(own, own_ref[r].astype(F32), oth_ref[r].astype(F32))
            out[r] = picked.astype(BF16)


def settle_rows(at_ref, parent_ref, s0, s1, s2, s3, ssm_ref, conv_ref):
    rows = s0.shape[0]
    y, c = at_ref[0], at_ref[1]
    for r in range(rows):
        parent = parent_ref[(2 * y + c) * rows + r]
        slot = lax.rem(lax.div(parent, 2) + 4 - y, 4)
        row = s0[r].astype(F32)
        for k, ref in ((1, s1), (2, s2), (3, s3)):
            row = jnp.where(slot == k, ref[r].astype(F32), row)
        ssm_ref[r] = row[:STATE_DIM]
        conv_ref[r] = row[STATE_DIM:].astype(BF16)


def project_in(columns, h_ref, gain_ref, w_ref, out_ref, scr):
    wide = w_ref.shape[1]
    rows = out_ref.shape[1]
    sides = 4
    chan = (out_ref.shape[2] - TAIL) // (sides + 1)
    hidden = h_ref[...]
    normed = (hidden * gain_ref[...]).astype(BF16)
    squares = jnp.sum(hidden * hidden, axis=1, keepdims=True)
    high = squares.astype(BF16).astype(F32)
    lane = lax.broadcasted_iota(jnp.int32, (hidden.shape[0], TAIL), 1)
    scr[:, wide:] = jnp.where(lane == 0, high, jnp.where(lane == 1, squares - high, 0.0))
    for at in range(0, wide, columns):
        there = slice(at, at + columns)
        scr[:, there] = jnp.dot(normed, w_ref[:, there], preferred_element_type=F32)
    for y in range(out_ref.shape[0] // sides):
        own = slice(y * rows, (y + 1) * rows)
        for v in range(sides):
            place = y * sides + v
            for j in range(sides):
                at = ((v - j) % sides) * chan
                out_ref[place, :, j * chan : (j + 1) * chan] = scr[own, at : at + chan].astype(BF16)
            at = (sides + v) * chan
            there = slice(sides * chan, (sides + 1) * chan)
            out_ref[place, :, there] = scr[own, at : at + chan].astype(BF16)
            out_ref[place, :, (sides + 1) * chan :] = scr[own, wide:].astype(BF16)


def advance(
    section, model_width, at_ref, sums_ref, small_ref, c0, c1, c2, c3, x0, x1, x2, x3, w_dt, x_in,
    ssm_in,
    mixed_ref, x_out, ssm_out, scr,
):
    total = sums_ref[0].astype(F32)
    for i in range(1, sums_ref.shape[0]):
        total = total + sums_ref[i].astype(F32)
    rows = total.shape[0]
    chan = w_dt.shape[1]
    wide = total.shape[1] - TAIL
    squares = total[:, wide : wide + 1] + total[:, wide + 1 : wide + 2]
    scale = lax.rsqrt(squares / model_width + EPSILON)
    projected = (total[:, :wide] * scale).astype(BF16).astype(F32)
    acts = []
    low = jnp.zeros((rows, x0.shape[1]), F32)
    bc = jnp.zeros((rows, 2 * STATE_DIM), F32)
    for j, (conv, w) in enumerate(zip((c0, c1, c2, c3), (x0, x1, x2, x3))):
        x = projected[:, j * chan : (j + 1) * chan]
        acts.append(jax.nn.silu(conv[0:rows, :] + x * conv[rows : rows + 1, :]))
        act_half = acts[j].astype(BF16)
        low = low + jnp.dot(act_half, w[...], preferred_element_type=F32)
        bc = bc + lax.dot_general(
            act_half,
            conv[PAD:, :].astype(BF16),
            (((1,), (1,)), ((), ())),
            preferred_element_type=F32,
        )
    act = acts[0]
    gate = jax.nn.silu(projected[:, wide - chan :])
    pre = jnp.dot(low.astype(BF16), w_dt[...], preferred_element_type=F32)
    pre = pre + small_ref[rows + 1 : rows + 2, :]
    step = jnp.maximum(pre, 0.0) + jnp.log1p(jnp.exp(-jnp.abs(pre)))
    scr[0] = step
    scr[1] = step * act
    shape = (STATE_DIM, 2 * STATE_DIM)
    lane = lax.broadcasted_iota(jnp.int32, shape, 1)
    sub = lax.broadcasted_iota(jnp.int32, shape, 0)
    rates = small_ref[PAD:, :]
    live = at_ref[3] == section
    for g in range(rows):
        line = jnp.broadcast_to(bc[g : g + 1, :], shape)
        b_col = jnp.sum(jnp.where(lane == sub, line, 0.0), axis=1, keepdims=True)
        c_col = jnp.sum(jnp.where(lane == sub + STATE_DIM, line, 0.0), axis=1, keepdims=True)
        old = ssm_in[g]
        new = jnp.exp(-scr[0, g : g + 1, :] * rates) * old + b_col * scr[1, g : g + 1, :]
        scr[2, g : g + 1, :] = jnp.sum(c_col * new, axis=0, keepdims=True)
        ssm_out[g] = jnp.where(live, new, old)
    x_out[...] = jnp.where(live, projected[:, :chan], x_in[...])
    mixed = (scr[2] + small_ref[rows + 2 : rows + 3, :] * act) * gate
    mixed = mixed.astype(BF16)
    for i in range(mixed_ref.shape[0]):
        mixed_ref[i] = mixed


def project_out(sides, m_ref, h_ref, w_ref, out_ref, scr):
    rows, chan = m_ref.shape[1:]
    total = h_ref[...]
    for v in range(sides):
        for y in range(m_ref.shape[0] // sides):
            scr[y * rows : (y + 1) * rows, :] = m_ref[y * sides + v].astype(F32)
        total = total + jnp.dot(
            scr[...].astype(BF16),
            w_ref[v * chan : (v + 1) * chan, :],
            preferred_element_type=F32,
        )
    out_ref[...] = total


def finish(at_ref, h_ref, gain_ref, out_ref):
    rows = h_ref[...]
    width = rows.shape[1]
    half = width // 2
    first = at_ref[1] == 0
    left = jnp.where(first, rows[:, :half], rows[:, half:])
    right = jnp.where(first, rows[:, half:], rows[:, :half])
    out_ref[:, :half] = (left * gain_ref[:, :half]).astype(BF16)
    out_ref[:, half:width] = (right * gain_ref[:, half:]).astype(BF16)
    squares = jnp.sum(rows * rows, axis=1, keepdims=True)
    high = squares.astype(BF16).astype(F32)
    lane = lax.broadcasted_iota(jnp.int32, (rows.shape[0], TAIL), 1)
    tail = jnp.where(lane == 0, high, jnp.where(lane == 1, squares - high, 0.0))
    out_ref[:, width:] = tail.astype(BF16)


def local_call(body, outs, scratch=(), smem=0, operands=0, aliases=None, cost=None):
    specs = [whole(pltpu.SMEM)] * smem + [whole()] * (operands - smem)
    return pl.pallas_call(
        body,
        out_shape=[jax.ShapeDtypeStruct(shape, dtype) for shape, dtype in outs],
        in_specs=specs,
        out_specs=[whole()] * len(outs),
        scratch_shapes=[pltpu.VMEM(shape, F32) for shape in scratch],
        input_output_aliases=aliases or {},
        compiler_params=pltpu.CompilerParams(vmem_limit_bytes=12 * 2**20),
        cost_estimate=cost,
    )


def on_device(
    tokens_in,
    picks,
    parents,
    scores,
    embed,
    norm_gain,
    in_weight,
    conv_weight,
    conv_bias,
    xdt_weight,
    xbc_weight,
    dt_weight,
    dt_bias,
    a_rate,
    skip,
    out_weight,
    final_gain,
    head,
    conv_state,
    ssm_state,
):
    section_count = lax.axis_size("section")
    dp_count = lax.axis_size("dp")
    vocab_count = lax.axis_size("vocab")
    y_count = dp_count // 2
    row_total = tokens_in.shape[0]
    own_rows = row_total // dp_count
    core_rows = own_rows * y_count
    section_at = lax.axis_index("section")
    dp_at = lax.axis_index("dp")
    vocab_at = lax.axis_index("vocab")
    y_at = dp_at // 2
    core_at = dp_at % 2
    block = in_weight.shape[1]
    chan = in_weight.shape[3] // vocab_count
    model_width = final_gain.shape[0]
    pair_width = 2 * block
    sides = y_count * vocab_count
    vocab_rows = head.shape[0]

    coords = jnp.stack([y_at, core_at, vocab_at, section_at]).astype(jnp.int32)

    embed_rows = embed.shape[0]
    local_ids = tokens_in - section_at * embed_rows
    inside = (local_ids >= 0) & (local_ids < embed_rows)
    found = jnp.take(embed, jnp.clip(local_ids, 0, embed_rows - 1), axis=0)
    found = jnp.where(inside[:, None], found, 0).astype(BF16)
    found, in_own, ssm_now = lax.optimization_barrier((found, in_weight[0], ssm_state[0]))
    copies = jnp.broadcast_to(found[None], (section_count,) + found.shape)
    pieces = lax.all_to_all(copies, "section", 0, 0, tiled=True)
    looked_up = jnp.sum(pieces.astype(F32), axis=0).reshape(dp_count, own_rows, block)
    beside = jnp.pad(norm_gain, ((0, own_rows - 1), (0, 0)))
    bundle = jnp.concatenate([looked_up, beside[None]], axis=0)
    hidden, gain = local_call(
        lambda *refs: place_rows(dp_count, *refs),
        [((core_rows, pair_width), F32), ((1, pair_width), F32)],
        smem=1,
        operands=3,
    )(coords, bundle, other_core(bundle))

    in_own = in_own.reshape(block, 2 * vocab_count * chan)
    w_in = jnp.concatenate([in_own, other_core(in_own)], axis=0)
    w_out = jnp.concatenate([out_weight[0], other_core(out_weight[0])], axis=1)

    w_dt = dt_weight[0]
    _, taps, w_x = lax.optimization_barrier((pieces, conv_weight[0], xdt_weight[0]))
    conv_old = conv_state[0]
    keep = taps.shape[0] - 1
    conv_pre = conv_bias + jnp.sum(conv_old.astype(F32) * taps[None, :keep], axis=1)
    small = jnp.concatenate(
        [conv_pre, taps[keep:], dt_bias, skip, jnp.zeros((1, chan), F32), a_rate[0]], axis=0
    )
    x_kept = jnp.zeros((own_rows, chan), F32)

    wide = (vocab_count + 1) * chan + TAIL
    conv_rows = jnp.concatenate([small[:PAD], jnp.transpose(xbc_weight[0]).astype(F32)], axis=0)
    all_x = [w_x] + [by_vocab(w_x, k) for k in range(1, vocab_count)]
    all_conv = [conv_rows] + [by_vocab(conv_rows, k) for k in range(1, vocab_count)]
    call_in = local_call(
        lambda *refs: project_in(512, *refs),
        [((sides, own_rows, wide), BF16)],
        scratch=[(core_rows, 2 * vocab_count * chan + TAIL)],
        operands=3,
        cost=pl.CostEstimate(
            flops=4 * core_rows * pair_width * vocab_count * chan,
            bytes_accessed=4 * pair_width * vocab_count * chan,
            transcendentals=0,
        ),
    )
    def call_state(section, *operands):
        return local_call(
            lambda *refs: advance(section, model_width, *refs),
            [((sides, own_rows, chan), BF16), ((own_rows, chan), F32), (ssm_now.shape, F32)],
            scratch=[(3, own_rows, chan)],
            smem=1,
            operands=14,
            aliases={12: 1, 13: 2},
            cost=pl.CostEstimate(
                flops=10 * own_rows * chan * dt_weight.shape[1],
                bytes_accessed=10 * chan * dt_weight.shape[1] + 8 * ssm_now.size,
                transcendentals=ssm_now.size,
            ),
        )(*operands)

    call_out = local_call(
        lambda *refs: project_out(vocab_count, *refs),
        [((core_rows, pair_width), F32)],
        scratch=[(core_rows, chan)],
        operands=3,
        cost=pl.CostEstimate(
            flops=2 * core_rows * pair_width * vocab_count * chan,
            bytes_accessed=2 * pair_width * vocab_count * chan,
            transcendentals=0,
        ),
    )

    for step in range(section_count):
        (parts,) = call_in(hidden, gain, w_in)
        if step == 0:
            _, all_x, all_conv, w_out = lax.optimization_barrier((parts, all_x, all_conv, w_out))
        mixed, x_kept, ssm_now = call_state(
            step, coords, over_side(parts), small, *all_conv, *all_x, w_dt, x_kept, ssm_now
        )
        (hidden,) = call_out(over_side(mixed), hidden, w_out)
        if step + 1 < section_count:
            hidden = next_section(hidden)

    pair_gain = final_gain.reshape(y_count, 2, vocab_count, block)
    pair_gain = lax.dynamic_index_in_dim(pair_gain, y_at, 0, keepdims=False)
    pair_gain = lax.dynamic_index_in_dim(pair_gain, vocab_at, 1, keepdims=False)
    (sent,) = local_call(
        finish,
        [((core_rows, pair_width + TAIL), BF16)],
        smem=1,
        operands=3,
    )(coords, hidden, pair_gain.reshape(1, pair_width))
    last = section_count - 1
    middle = last // 2
    got = lax.ppermute(sent, "section", [(last, middle)])
    sent = jnp.where(section_at == middle, got, sent)
    received = jnp.zeros_like(sent)
    for k in range(1, middle + 1):
        pairs = [(last, (last + k) % section_count), (middle, middle + k)]
        received = received + lax.ppermute(sent, "section", pairs)
    _, ssm_now, x_kept = lax.optimization_barrier((got, ssm_now, x_kept))
    conv_next = jnp.concatenate([conv_old[:, 1:], x_kept.astype(BF16)[:, None]], axis=1)
    states = jnp.concatenate([ssm_now.astype(BF16), conv_next], axis=1)
    chosen = local_call(
        choose_rows,
        [(states.shape, BF16)] * y_count,
        smem=2,
        operands=4,
    )(coords, parents[0], states, other_core(states))
    chosen = [chosen[0]] + [by_y(chosen[k], -k) for k in range(1, y_count)]
    ssm_new, conv_new = local_call(
        settle_rows,
        [(ssm_now.shape, F32), (conv_next.shape, BF16)],
        smem=2,
        operands=6,
    )(coords, parents[0], *chosen)
    is_source = (section_at == middle) | (section_at == last)
    sent = jnp.where(is_source, sent, received)
    every = over_side(jnp.broadcast_to(sent[None], (sides,) + sent.shape))
    facing = other_core(every)
    cores = jnp.where(core_at == 0, jnp.stack([every, facing]), jnp.stack([facing, every]))
    cores = cores.reshape(2, y_count, vocab_count, y_count, own_rows, pair_width + TAIL)
    sums = jnp.sum(cores[..., pair_width : pair_width + 2].astype(F32), axis=(1, 2, 5))
    sums = jnp.transpose(sums, (1, 0, 2)).reshape(row_total)
    final = cores[..., :pair_width].reshape(2, y_count, vocab_count, y_count, own_rows, 2, block)
    final = jnp.transpose(final, (3, 0, 4, 1, 5, 2, 6)).reshape(row_total, model_width)
    final_scale = lax.rsqrt(sums / model_width + EPSILON)
    logits = lax.dot_general(final, head, (((1,), (1,)), ((), ())), preferred_element_type=F32)
    logits = logits * final_scale[:, None]

    source_of = jnp.arange(row_total, dtype=jnp.int32) % SOURCES
    parent_row = parents[0] * SOURCES + source_of
    vocab_offset = lax.axis_index(("section", "dp", "vocab")) * vocab_rows
    parent_logits = jnp.take(logits, parent_row, axis=0)
    is_pick = jnp.arange(vocab_rows, dtype=jnp.int32)[None, :] + vocab_offset == picks[0][:, None]
    picked = jnp.sum(jnp.where(is_pick, parent_logits, 0.0), axis=1)
    top = jnp.max(logits, axis=1)
    total = jnp.sum(jnp.exp(logits - top[:, None]), axis=1)
    for axes in (("dp", "vocab"), ("section",)):
        stats = jnp.stack([top, total, picked] + [jnp.zeros_like(top)] * 5)
        stats = jnp.pad(stats, ((0, 0), (0, 128 - row_total)))
        copies = jnp.broadcast_to(stats[None], (lax.axis_size(axes),) + stats.shape)
        every = lax.all_to_all(copies, axes, 0, 0, tiled=True)[:, :, :row_total]
        tops, totals, picks_of = every[:, 0], every[:, 1], every[:, 2]
        top = jnp.max(tops, axis=0)
        total = jnp.sum(totals * jnp.exp(tops - top[None]), axis=0)
        picked = jnp.sum(picks_of, axis=0)
    log_norm = top + jnp.log(total)
    scores_now = jnp.take(scores, parent_row) + picked - jnp.take(log_norm, parent_row)

    return (conv_new[None], ssm_new[None], scores_now)


def solution(mesh):
    placed = (
        P(),
        P(),
        P(),
        P(),
        P("section", ("dp", "vocab")),
        P("section", ("dp", "vocab")),
        P("section", ("dp", "vocab"), None, None),
        P("section", None, "vocab"),
        P("section", "vocab"),
        P("section", "vocab", None),
        P("section", "vocab", None),
        P("section", None, "vocab"),
        P("section", "vocab"),
        P("section", None, "vocab"),
        P("section", "vocab"),
        P("section", None, ("dp", "vocab")),
        P(),
        P(("section", "dp", "vocab"), None),
        P("section", "dp", None, "vocab"),
        P("section", "dp", None, "vocab"),
    )
    return jax.shard_map(
        on_device,
        mesh=mesh,
        in_specs=placed,
        out_specs=(P("section", "dp", None, "vocab"), P("section", "dp", None, "vocab"), P()),
        check_vma=False,
    )
```
